32 devices in a mesh: lat: 2 (over x), lon: 16 (over z, y, core).
Axes of the slice: x: 2, y: 2, z: 4, core: 2. Of those that a mesh axis runs over, the one named last changes fastest.
Arguments:
- tracer: float32 [4, 512, 2048], P(None, 'lat', 'lon'), may hold values from -6 to 6
- wind_east: float32 [4, 512, 2048], P(None, 'lat', 'lon'), may hold values from -4 to 4
- wind_north: float32 [4, 512, 2048], P(None, 'lat', 'lon'), may hold values from -4 to 4
- kappa: float32 [4, 512, 2048], P(None, 'lat', 'lon'), may hold values from 0.25 to 4
- cutoff: int32 [128], replicated, may hold values from 64 to 511
- partner: int32 [2048], replicated, may hold values from 0 to 2047, as said below
Outputs:
- filtered: float32 [4, 512, 2048], P(None, 'lat', 'lon')
- balanced: float32 [4, 512, 2048], P(None, 'lat', 'lon')
The draws below stay inside these ranges and needn't reach their ends.
Inputs may be any that keep to these rules, and one draw needn't show every extreme that they name: partner[j] = (j + 1024 + s_j) mod 2048 with each column's own shift s_j of 0 to 127; some column has s_j = 127.
All inputs are finite; a program needn't handle non-finite values.
Results may differ from the reference program's by a relative error of at most 0.00005.
Values sent between devices are 32-bit elements; how exact they have to be, the bound alone decides.
A program may use at most 64 MiB of HBM per device.

```python
import math
import jax
import jax.numpy as jnp

CLON = 128
LEV = 4
POLE = 64
KMAX = 512
SWEEPS = 4
NLON = 2048
NLAT = 512


def draw_partner(key, part):
    shifts = jax.random.randint(jax.random.fold_in(key, 7), (NLON,), 0, CLON, dtype=jnp.int32)
    shifts = shifts.at[NLON // 2 - 1].set(0)
    shifts = shifts.at[NLON // 2].set(0)
    shifts = shifts.at[1].set(CLON - 1)
    columns = jnp.arange(NLON, dtype=jnp.int32)
    return ((columns + NLON // 2 + shifts) % NLON).astype(jnp.int32)


def draw_cutoff(key, part):
    lowest = KMAX // 8
    values = jax.random.randint(jax.random.fold_in(key, 1), (2 * POLE,), lowest, KMAX, dtype=jnp.int32)
    first = jax.random.randint(jax.random.fold_in(key, 2), (), 0, 2 * POLE, dtype=jnp.int32)
    offset = jax.random.randint(jax.random.fold_in(key, 3), (), 1, 2 * POLE, dtype=jnp.int32)
    second = (first + offset) % (2 * POLE)
    values = values.at[first].set(KMAX - 1)
    values = values.at[second].set(lowest)
    return values.astype(jnp.int32)


def block_scale(rng, extent, pieces, least, high):
    factor_of, own = 1.0, jax.random.fold_in(rng, 6)
    for axis_at, shards_of in pieces:
        draws = jnp.exp(jax.random.uniform(jax.random.fold_in(own, axis_at), (shards_of,), jnp.float32, least / len(pieces), high / len(pieces)))
        factor_of = factor_of * jnp.repeat(draws, extent[axis_at] // shards_of).reshape([-1 if axis == axis_at else 1 for axis in range(len(extent))])
    return factor_of


def centred(key, shape, width, reach, shards=(), held_as=jnp.bfloat16):
    result = width * jax.random.normal(key, shape, jnp.float32)
    if shards:
        result = result * block_scale(key, shape, shards, -0.22, 0.18)
    return jnp.clip(result, -reach, reach).astype(held_as)


def setup_inputs(seed: int = 0) -> dict:
    key_list = jax.random.split(jax.random.key(seed), 7)
    tracer = centred(key_list[0], (LEV, NLAT, NLON), 1.0, 6.0, ((1, 2), (2, 16)), jnp.float32)
    wind_east = centred(key_list[1], (LEV, NLAT, NLON), 1.0, 4.0, ((1, 2), (2, 16)), jnp.float32)
    wind_north = centred(key_list[2], (LEV, NLAT, NLON), 1.0, 4.0, ((1, 2), (2, 16)), jnp.float32)
    kappa = jnp.clip(jnp.exp(math.log(4.0) - 2.7725887 * jax.random.uniform(key_list[3], (LEV, NLAT, NLON), jnp.float32) ** block_scale(key_list[3], (LEV, NLAT, NLON), ((1, 2), (2, 16)), -0.2, 0.2)), 0.25, 4.0)
    cutoff = draw_cutoff(jax.random.fold_in(key_list[6], 71), 0)
    partner = draw_partner(jax.random.fold_in(key_list[6], 71), 0)
    return {"tracer": tracer, "wind_east": wind_east, "wind_north": wind_north, "kappa": kappa, "cutoff": cutoff, "partner": partner}


COURANT = 0.4


def neighbours(field, partner):
    beyond_north = jnp.take(field[:, 0, :], partner, axis=1)
    beyond_south = jnp.take(field[:, -1, :], partner, axis=1)
    upper = jnp.concatenate([beyond_north[:, None, :], field[:, :-1, :]], axis=1)
    lower = jnp.concatenate([field[:, 1:, :], beyond_south[:, None, :]], axis=1)
    western = jnp.roll(field, 1, axis=2)
    eastern = jnp.roll(field, -1, axis=2)
    return western, eastern, upper, lower


def lowpass(rows, limits):
    spectrum = jnp.fft.rfft(rows, axis=-1)
    waves = jnp.arange(spectrum.shape[-1], dtype=jnp.int32)
    keep = waves[None, None, :] <= limits[None, :, None]
    spectrum = jnp.where(keep, spectrum, 0.0)
    return jnp.fft.irfft(spectrum, n=rows.shape[-1], axis=-1).astype(rows.dtype)


def reference(tracer, wind_east, wind_north, kappa, cutoff, partner):
    western, eastern, upper, lower = neighbours(tracer, partner)
    advected = tracer - COURANT * 0.5 * (wind_east * (eastern - western) + wind_north * (lower - upper))
    north_rows = lowpass(advected[:, :POLE, :], cutoff[:POLE])
    south_rows = lowpass(advected[:, NLAT - POLE:, :], cutoff[POLE:])
    filtered = jnp.concatenate([north_rows, advected[:, POLE:NLAT - POLE, :], south_rows], axis=1)
    balanced = filtered
    for sweep_index in range(SWEEPS):
        western, eastern, upper, lower = neighbours(balanced, partner)
        balanced = (filtered + kappa * (western + eastern + upper + lower)) / (1.0 + 4.0 * kappa)
    return filtered, balanced
```

```python
import functools
import math

import jax
import jax.numpy as jnp
import numpy as np
from jax import lax
from jax.experimental import pallas as pl
from jax.experimental.pallas import tpu as pltpu
from jax.sharding import PartitionSpec as P

KMAX = 512
SWEEPS = 4
COURANT = 0.4
HIGHEST = lax.Precision.HIGHEST


def tables(sectors, width):
    total = sectors * width
    half = sectors // 2
    m = np.arange(width)
    theta = 2.0 * np.pi * (np.outer(np.arange(half + 1), m) % total) / total
    kept = 2 * KMAX // sectors
    k2 = np.arange(kept) - kept // 2
    phase = 2.0 * np.pi * (np.outer(m, k2) % width) / width
    c, s = np.cos(phase), np.sin(phase)
    forward = np.block([[c, -s], [s, c]])
    inverse = np.block([[c.T, s.T], [-s.T, c.T]]) / total
    return [a.astype(np.float32) for a in (np.cos(theta), np.sin(theta), forward, inverse)]


def weighted(terms):
    total = None
    for factor, value in terms:
        if abs(factor) < 1e-12:
            continue
        part = value if abs(factor - 1.0) < 1e-12 else value * np.float32(factor)
        total = part if total is None else total + part
    return total


def kernel(
    sectors, bands,
    tracer, wind_east, wind_north, kappa, cutoff, partner, tw_cos, tw_sin, fwd, inv,
    filtered, balanced,
    col_send, col_recv, edge_send, edge_recv, spread, send_b, recv_b, coupling, scaled, ping, pong,
    halo_ss, halo_rs, a_ss, a_rs, b_ss, b_rs,
):
    lev, rows, width = tracer.shape
    pole = cutoff.shape[1] // 2
    share = lev * pole // sectors
    slices = sectors // lev
    half = sectors // 2
    groups = lev * rows // 8
    per = rows // 8
    lat = lax.axis_index("lat")
    lon = lax.axis_index("lon")

    def sector(offset):
        return lax.rem(lon + (offset % sectors), sectors)

    def band(offset):
        return lax.rem(lat + (offset % bands), bands)

    barrier = pltpu.get_barrier_semaphore()
    for t in range(1, sectors):
        pl.semaphore_signal(barrier, inc=1, device_id=(lat, sector(t)), device_id_type=pl.DeviceIdType.MESH)
    for t in (1, -1):
        pl.semaphore_signal(barrier, inc=1, device_id=(band(t), lon), device_id_type=pl.DeviceIdType.MESH)
    pl.semaphore_wait(barrier, sectors + 1)

    lane2 = lax.broadcasted_iota(jnp.int32, (rows, width), 1)
    row2 = lax.broadcasted_iota(jnp.int32, (rows, width), 0)
    diagonal = lax.broadcasted_iota(jnp.int32, (groups, 8, width), 0) == lax.broadcasted_iota(
        jnp.int32, (groups, 8, width), 2
    )
    reach = partner[pl.ds(lon, 1), :] - sector(half) * width
    reach = jnp.where(reach < 0, reach + sectors * width, reach)
    pick = jnp.where(
        lax.broadcasted_iota(jnp.int32, (2 * width, width), 0) == reach, 1.0, 0.0
    ).astype(jnp.float32)

    def post(turn, field):
        whole = field[...].reshape(groups, 8, width)
        col_send[turn, 0] = jnp.sum(jnp.where(diagonal, whole[:, :, width - 1 : width], 0.0), axis=0)
        col_send[turn, 1] = jnp.sum(jnp.where(diagonal, whole[:, :, 0:1], 0.0), axis=0)
        for l in range(lev):
            edge_send[turn, l : l + 1, :] = field[l, 0:1, :]
            edge_send[turn, lev + l : lev + l + 1, :] = field[l, rows - 1 : rows, :]
        plan = [
            (edge_send.at[turn], edge_recv.at[turn, 0], (lat, sector(-half))),
            (edge_send.at[turn], edge_recv.at[turn, 1], (lat, sector(-half - 1))),
            (edge_send.at[turn], edge_recv.at[turn, 2], (band(1), lon)),
            (edge_send.at[turn], edge_recv.at[turn, 3], (band(-1), lon)),
            (col_send.at[turn, 0], col_recv.at[turn, 0], (lat, sector(1))),
            (col_send.at[turn, 1], col_recv.at[turn, 1], (lat, sector(-1))),
        ]
        copies = []
        for i, (src, dst, device) in enumerate(plan):
            copy = pltpu.make_async_remote_copy(
                src_ref=src, dst_ref=dst, send_sem=halo_ss.at[turn, i], recv_sem=halo_rs.at[turn, i],
                device_id=device, device_id_type=pl.DeviceIdType.MESH,
            )
            copy.start()
            copies.append(copy)
        return copies

    def sides(turn):
        across = jnp.dot(
            jnp.concatenate([edge_recv[turn, 0], edge_recv[turn, 1]], axis=1), pick,
            precision=HIGHEST, preferred_element_type=jnp.float32,
        )
        top = jnp.where(lat == 0, across[:lev], edge_recv[turn, 2, lev:])
        bottom = jnp.where(lat == bands - 1, across[lev:], edge_recv[turn, 3, :lev])
        west = jnp.sum(jnp.where(diagonal, col_recv[turn, 0][None], 0.0), axis=2, keepdims=True)
        east = jnp.sum(jnp.where(diagonal, col_recv[turn, 1][None], 0.0), axis=2, keepdims=True)
        return top, bottom, west, east

    def around(field, l, edges):
        top, bottom, west, east = edges
        x = field[l]
        w = jnp.broadcast_to(west[per * l : per * (l + 1)], (per, 8, width)).reshape(rows, width)
        e = jnp.broadcast_to(east[per * l : per * (l + 1)], (per, 8, width)).reshape(rows, width)
        return (
            jnp.where(lane2 == 0, w, pltpu.roll(x, 1, 1)),
            jnp.where(lane2 == width - 1, e, pltpu.roll(x, width - 1, 1)),
            jnp.where(row2 == 0, top[l : l + 1], pltpu.roll(x, 1, 0)),
            jnp.where(row2 == rows - 1, bottom[l : l + 1], pltpu.roll(x, rows - 1, 0)),
        )

    copies = post(0, tracer)
    for l in range(lev):
        coupling[l] = kappa[l] / (1.0 + 4.0 * kappa[l])
    for copy in copies:
        copy.wait()
    edges = sides(0)
    for l in range(lev):
        w, e, u, d = around(tracer, l, edges)
        filtered[l] = tracer[l] - COURANT * 0.5 * (wind_east[l] * (e - w) + wind_north[l] * (d - u))

    base = jnp.where(lat == bands - 1, rows - pole, 0)

    def part(device):
        return lax.div(device, slices), pl.ds(pl.multiple_of(base + lax.rem(device, slices) * share, 8), share)

    copies = []
    for t in range(1, sectors):
        level, span = part(sector(t))
        copy = pltpu.make_async_remote_copy(
            src_ref=filtered.at[level, span, :], dst_ref=spread.at[lon],
            send_sem=a_ss.at[t], recv_sem=a_rs.at[t],
            device_id=(lat, sector(t)), device_id_type=pl.DeviceIdType.MESH,
        )
        copy.start()
        copies.append(copy)
    level, span = part(lon)
    spread[lon] = filtered[level, span, :]

    first = jnp.where(lat == bands - 1, pole, 0) + lax.rem(lon, slices) * share
    spot = lax.broadcasted_iota(jnp.int32, (share, 2 * pole), 0) + first
    limit = jnp.sum(
        jnp.where(
            lax.broadcasted_iota(jnp.int32, (share, 2 * pole), 1) == spot,
            cutoff[...].astype(jnp.float32), 0.0,
        ),
        axis=1, keepdims=True,
    )
    kept = 2 * KMAX // sectors
    slot = lax.broadcasted_iota(jnp.int32, (share, 2 * kept), 1)
    wave = sectors * (jnp.where(slot < kept, slot, slot - kept) - kept // 2)
    for copy in copies:
        copy.wait()

    def circle(d, k):
        angle = 2.0 * math.pi * ((d * k) % sectors) / sectors
        return math.cos(angle), math.sin(angle)

    even = [spread[0]] + [spread[d] + spread[sectors - d] for d in range(1, half)] + [spread[half]]
    odd = [None] + [spread[d] - spread[sectors - d] for d in range(1, half)]
    blocks = []
    for k in range(half + 1):
        c, s = tw_cos[k : k + 1, :], tw_sin[k : k + 1, :]
        re = weighted([(circle(d, k)[0], even[d]) for d in range(half + 1)])
        im = weighted([(-circle(d, k)[1], odd[d]) for d in range(1, half)])
        if im is None:
            blocks.append(jnp.concatenate([re * c, -(re * s)], axis=1))
        else:
            blocks.append(jnp.concatenate([re * c + im * s, im * c - re * s], axis=1))
    spectrum = jnp.dot(
        jnp.concatenate(blocks, axis=0), fwd[...], precision=HIGHEST, preferred_element_type=jnp.float32
    )
    keep = jnp.concatenate(
        [jnp.where(jnp.abs(wave + k).astype(jnp.float32) <= limit, 1.0, 0.0) for k in range(half + 1)], axis=0
    )
    back = jnp.dot(
        jnp.where(keep > 0.0, spectrum, 0.0), inv[...], precision=HIGHEST, preferred_element_type=jnp.float32
    )
    real, imag = [], []
    for k in range(half + 1):
        c, s = tw_cos[k : k + 1, :], tw_sin[k : k + 1, :]
        zr = back[k * share : (k + 1) * share, :width]
        zi = back[k * share : (k + 1) * share, width:]
        twice = 1.0 if k in (0, half) else 2.0
        real.append((zr * c - zi * s) * twice)
        imag.append((zr * s + zi * c) * twice)
    for d in range(half + 1):
        p = weighted([(circle(d, k)[0], real[k]) for k in range(half + 1)])
        q = weighted([(circle(d, k)[1], imag[k]) for k in range(1, half)])
        if q is None:
            send_b[d] = p
        else:
            send_b[d] = p - q
            send_b[sectors - d] = p + q

    copies = []
    for t in range(1, sectors):
        copy = pltpu.make_async_remote_copy(
            src_ref=send_b.at[sector(t)], dst_ref=recv_b.at[lon],
            send_sem=b_ss.at[t], recv_sem=b_rs.at[t],
            device_id=(lat, sector(t)), device_id_type=pl.DeviceIdType.MESH,
        )
        copy.start()
        copies.append(copy)
    recv_b[lon] = send_b[lon]
    for copy in copies:
        copy.wait()

    def restore(start):
        for l in range(lev):
            for q in range(slices):
                filtered[l, start + q * share : start + (q + 1) * share, :] = recv_b[l * slices + q]

    @pl.when(lat == 0)
    def _():
        restore(0)

    @pl.when(lat == bands - 1)
    def _():
        restore(rows - pole)

    chain = [filtered, ping, pong, ping, balanced]
    for sweep in range(SWEEPS):
        source, target = chain[sweep], chain[sweep + 1]
        copies = post(1 + sweep, source)
        if sweep == 0:
            for l in range(lev):
                scaled[l] = filtered[l] / (1.0 + 4.0 * kappa[l])
        for copy in copies:
            copy.wait()
        edges = sides(1 + sweep)
        for l in range(lev):
            w, e, u, d = around(source, l, edges)
            target[l] = scaled[l] + coupling[l] * (w + e + u + d)


def solution(mesh):
    sectors, bands = mesh.shape["lon"], mesh.shape["lat"]

    def per_device(tracer, wind_east, wind_north, kappa, cutoff, partner):
        lev, rows, width = tracer.shape
        share = lev * (cutoff.shape[0] // 2) // sectors
        turns = SWEEPS + 1
        block = pltpu.VMEM((lev, rows, width), jnp.float32)
        vmem = pl.BlockSpec(memory_space=pltpu.VMEM)
        return pl.pallas_call(
            functools.partial(kernel, sectors, bands),
            out_shape=[jax.ShapeDtypeStruct(tracer.shape, jnp.float32)] * 2,
            in_specs=[vmem] * 10,
            out_specs=[vmem] * 2,
            scratch_shapes=[
                pltpu.VMEM((turns, 2, 8, width), jnp.float32),
                pltpu.VMEM((turns, 2, 8, width), jnp.float32),
                pltpu.VMEM((turns, 2 * lev, width), jnp.float32),
                pltpu.VMEM((turns, 4, 2 * lev, width), jnp.float32),
                pltpu.VMEM((sectors, share, width), jnp.float32),
                pltpu.VMEM((sectors, share, width), jnp.float32),
                pltpu.VMEM((sectors, share, width), jnp.float32),
                block, block, block, block,
                pltpu.SemaphoreType.DMA((turns, 6)),
                pltpu.SemaphoreType.DMA((turns, 6)),
                pltpu.SemaphoreType.DMA((sectors,)),
                pltpu.SemaphoreType.DMA((sectors,)),
                pltpu.SemaphoreType.DMA((sectors,)),
                pltpu.SemaphoreType.DMA((sectors,)),
            ],
            compiler_params=pltpu.CompilerParams(
                collective_id=0, has_side_effects=True, vmem_limit_bytes=32 * 1024 * 1024
            ),
        )(
            tracer, wind_east, wind_north, kappa,
            cutoff.reshape(1, -1), partner.reshape(sectors, width),
            *tables(sectors, width),
        )

    spec = P(None, "lat", "lon")
    return jax.shard_map(
        per_device, mesh=mesh, in_specs=(spec, spec, spec, spec, P(), P()), out_specs=(spec, spec),
        check_vma=False,
    )
```

```python
import functools
import math

import jax
import jax.numpy as jnp
import numpy as np
from jax import lax
from jax.experimental import pallas as pl
from jax.experimental.pallas import tpu as pltpu
from jax.sharding import PartitionSpec as P

KMAX = 512
SWEEPS = 4
COURANT = 0.4
HIGHEST = lax.Precision.HIGHEST


def tables(sectors, width):
    total = sectors * width
    half = sectors // 2
    m = np.arange(width)
    theta = 2.0 * np.pi * (np.outer(np.arange(half + 1), m) % total) / total
    kept = 2 * KMAX // sectors
    k2 = np.arange(kept) - kept // 2
    phase = 2.0 * np.pi * (np.outer(m, k2) % width) / width
    c, s = np.cos(phase), np.sin(phase)
    forward = np.block([[c, -s], [s, c]])
    inverse = np.block([[c.T, s.T], [-s.T, c.T]]) / total
    return [a.astype(np.float32) for a in (np.cos(theta), np.sin(theta), forward, inverse)]


def weighted(terms):
    total = None
    for factor, value in terms:
        if abs(factor) < 1e-12:
            continue
        part = value if abs(factor - 1.0) < 1e-12 else value * np.float32(factor)
        total = part if total is None else total + part
    return total


def kernel(
    sectors, bands,
    tracer_h, wind_east_h, wind_north_h, kappa_h, cutoff_h, partner_h, tw_cos_h, tw_sin_h, fwd_h, inv_h,
    filtered, balanced,
    tracer, wind_east, wind_north, kappa, cutoff, partner, tw_cos, tw_sin, fwd, inv, load_s,
    col_send, col_recv, edge_send, edge_recv, spread, send_b, recv_b, coupling, scaled, ping, pong,
    halo_ss, halo_rs, a_ss, a_rs, b_ss, b_rs,
):
    lev, rows, width = tracer.shape
    pole = cutoff.shape[1] // 2
    share = lev * pole // sectors
    slices = sectors // lev
    half = sectors // 2
    groups = lev * rows // 8
    per = rows // 8
    lat = lax.axis_index("lat")
    lon = lax.axis_index("lon")

    def sector(offset):
        return lax.rem(lon + (offset % sectors), sectors)

    def band(offset):
        return lax.rem(lat + (offset % bands), bands)

    held = (tracer_h, partner_h, wind_east_h, wind_north_h, kappa_h, cutoff_h, tw_cos_h, tw_sin_h, fwd_h, inv_h)
    near = (tracer, partner, wind_east, wind_north, kappa, cutoff, tw_cos, tw_sin, fwd, inv)
    loads = [pltpu.make_async_copy(h, v, load_s.at[i]) for i, (h, v) in enumerate(zip(held, near))]
    for load in loads:
        load.start()

    barrier = pltpu.get_barrier_semaphore()
    for t in range(1, sectors):
        pl.semaphore_signal(barrier, inc=1, device_id=(lat, sector(t)), device_id_type=pl.DeviceIdType.MESH)
    for t in (1, -1):
        pl.semaphore_signal(barrier, inc=1, device_id=(band(t), lon), device_id_type=pl.DeviceIdType.MESH)
    pl.semaphore_wait(barrier, sectors + 1)

    loads[0].wait()
    loads[1].wait()
    lane2 = lax.broadcasted_iota(jnp.int32, (rows, width), 1)
    row2 = lax.broadcasted_iota(jnp.int32, (rows, width), 0)
    diagonal = lax.broadcasted_iota(jnp.int32, (groups, 8, width), 0) == lax.broadcasted_iota(
        jnp.int32, (groups, 8, width), 2
    )
    reach = partner[pl.ds(lon, 1), :] - sector(half) * width
    reach = jnp.where(reach < 0, reach + sectors * width, reach)
    pick = jnp.where(
        lax.broadcasted_iota(jnp.int32, (2 * width, width), 0) == reach, 1.0, 0.0
    ).astype(jnp.float32)

    def post(turn, field):
        whole = field[...].reshape(groups, 8, width)
        col_send[turn, 0] = jnp.sum(jnp.where(diagonal, whole[:, :, width - 1 : width], 0.0), axis=0)
        col_send[turn, 1] = jnp.sum(jnp.where(diagonal, whole[:, :, 0:1], 0.0), axis=0)
        for l in range(lev):
            edge_send[turn, l : l + 1, :] = field[l, 0:1, :]
            edge_send[turn, lev + l : lev + l + 1, :] = field[l, rows - 1 : rows, :]
        plan = [
            (edge_send.at[turn], edge_recv.at[turn, 0], (lat, sector(-half))),
            (edge_send.at[turn], edge_recv.at[turn, 1], (lat, sector(-half - 1))),
            (edge_send.at[turn], edge_recv.at[turn, 2], (band(1), lon)),
            (edge_send.at[turn], edge_recv.at[turn, 3], (band(-1), lon)),
            (col_send.at[turn, 0], col_recv.at[turn, 0], (lat, sector(1))),
            (col_send.at[turn, 1], col_recv.at[turn, 1], (lat, sector(-1))),
        ]
        copies = []
        for i, (src, dst, device) in enumerate(plan):
            copy = pltpu.make_async_remote_copy(
                src_ref=src, dst_ref=dst, send_sem=halo_ss.at[turn, i], recv_sem=halo_rs.at[turn, i],
                device_id=device, device_id_type=pl.DeviceIdType.MESH,
            )
            copy.start()
            copies.append(copy)
        return copies

    def sides(turn):
        across = jnp.dot(
            jnp.concatenate([edge_recv[turn, 0], edge_recv[turn, 1]], axis=1), pick,
            precision=HIGHEST, preferred_element_type=jnp.float32,
        )
        top = jnp.where(lat == 0, across[:lev], edge_recv[turn, 2, lev:])
        bottom = jnp.where(lat == bands - 1, across[lev:], edge_recv[turn, 3, :lev])
        west = jnp.sum(jnp.where(diagonal, col_recv[turn, 0][None], 0.0), axis=2, keepdims=True)
        east = jnp.sum(jnp.where(diagonal, col_recv[turn, 1][None], 0.0), axis=2, keepdims=True)
        return top, bottom, west, east

    def around(field, l, edges):
        top, bottom, west, east = edges
        x = field[l]
        w = jnp.broadcast_to(west[per * l : per * (l + 1)], (per, 8, width)).reshape(rows, width)
        e = jnp.broadcast_to(east[per * l : per * (l + 1)], (per, 8, width)).reshape(rows, width)
        return (
            jnp.where(lane2 == 0, w, pltpu.roll(x, 1, 1)),
            jnp.where(lane2 == width - 1, e, pltpu.roll(x, width - 1, 1)),
            jnp.where(row2 == 0, top[l : l + 1], pltpu.roll(x, 1, 0)),
            jnp.where(row2 == rows - 1, bottom[l : l + 1], pltpu.roll(x, rows - 1, 0)),
        )

    copies = post(0, tracer)
    for load in loads[2:]:
        load.wait()
    for l in range(lev):
        coupling[l] = kappa[l] / (1.0 + 4.0 * kappa[l])
    for copy in copies:
        copy.wait()
    edges = sides(0)
    for l in range(lev):
        w, e, u, d = around(tracer, l, edges)
        filtered[l] = tracer[l] - COURANT * 0.5 * (wind_east[l] * (e - w) + wind_north[l] * (d - u))

    base = jnp.where(lat == bands - 1, rows - pole, 0)

    def part(device):
        return lax.div(device, slices), pl.ds(pl.multiple_of(base + lax.rem(device, slices) * share, 8), share)

    copies = []
    for t in range(1, sectors):
        level, span = part(sector(t))
        copy = pltpu.make_async_remote_copy(
            src_ref=filtered.at[level, span, :], dst_ref=spread.at[lon],
            send_sem=a_ss.at[t], recv_sem=a_rs.at[t],
            device_id=(lat, sector(t)), device_id_type=pl.DeviceIdType.MESH,
        )
        copy.start()
        copies.append(copy)
    level, span = part(lon)
    spread[lon] = filtered[level, span, :]

    first = jnp.where(lat == bands - 1, pole, 0) + lax.rem(lon, slices) * share
    spot = lax.broadcasted_iota(jnp.int32, (share, 2 * pole), 0) + first
    limit = jnp.sum(
        jnp.where(
            lax.broadcasted_iota(jnp.int32, (share, 2 * pole), 1) == spot,
            cutoff[...].astype(jnp.float32), 0.0,
        ),
        axis=1, keepdims=True,
    )
    kept = 2 * KMAX // sectors
    slot = lax.broadcasted_iota(jnp.int32, (share, 2 * kept), 1)
    wave = sectors * (jnp.where(slot < kept, slot, slot - kept) - kept // 2)
    for copy in copies:
        copy.wait()

    def circle(d, k):
        angle = 2.0 * math.pi * ((d * k) % sectors) / sectors
        return math.cos(angle), math.sin(angle)

    even = [spread[0]] + [spread[d] + spread[sectors - d] for d in range(1, half)] + [spread[half]]
    odd = [None] + [spread[d] - spread[sectors - d] for d in range(1, half)]
    blocks = []
    for k in range(half + 1):
        c, s = tw_cos[k : k + 1, :], tw_sin[k : k + 1, :]
        re = weighted([(circle(d, k)[0], even[d]) for d in range(half + 1)])
        im = weighted([(-circle(d, k)[1], odd[d]) for d in range(1, half)])
        if im is None:
            blocks.append(jnp.concatenate([re * c, -(re * s)], axis=1))
        else:
            blocks.append(jnp.concatenate([re * c + im * s, im * c - re * s], axis=1))
    spectrum = jnp.dot(
        jnp.concatenate(blocks, axis=0), fwd[...], precision=HIGHEST, preferred_element_type=jnp.float32
    )
    keep = jnp.concatenate(
        [jnp.where(jnp.abs(wave + k).astype(jnp.float32) <= limit, 1.0, 0.0) for k in range(half + 1)], axis=0
    )
    back = jnp.dot(
        jnp.where(keep > 0.0, spectrum, 0.0), inv[...], precision=HIGHEST, preferred_element_type=jnp.float32
    )
    real, imag = [], []
    for k in range(half + 1):
        c, s = tw_cos[k : k + 1, :], tw_sin[k : k + 1, :]
        zr = back[k * share : (k + 1) * share, :width]
        zi = back[k * share : (k + 1) * share, width:]
        twice = 1.0 if k in (0, half) else 2.0
        real.append((zr * c - zi * s) * twice)
        imag.append((zr * s + zi * c) * twice)
    for d in range(half + 1):
        p = weighted([(circle(d, k)[0], real[k]) for k in range(half + 1)])
        q = weighted([(circle(d, k)[1], imag[k]) for k in range(1, half)])
        if q is None:
            send_b[d] = p
        else:
            send_b[d] = p - q
            send_b[sectors - d] = p + q

    copies = []
    for t in range(1, sectors):
        copy = pltpu.make_async_remote_copy(
            src_ref=send_b.at[sector(t)], dst_ref=recv_b.at[lon],
            send_sem=b_ss.at[t], recv_sem=b_rs.at[t],
            device_id=(lat, sector(t)), device_id_type=pl.DeviceIdType.MESH,
        )
        copy.start()
        copies.append(copy)
    recv_b[lon] = send_b[lon]
    for copy in copies:
        copy.wait()

    def restore(start):
        for l in range(lev):
            for q in range(slices):
                filtered[l, start + q * share : start + (q + 1) * share, :] = recv_b[l * slices + q]

    @pl.when(lat == 0)
    def _():
        restore(0)

    @pl.when(lat == bands - 1)
    def _():
        restore(rows - pole)

    chain = [filtered, ping, pong, ping, balanced]
    for sweep in range(SWEEPS):
        source, target = chain[sweep], chain[sweep + 1]
        copies = post(1 + sweep, source)
        if sweep == 0:
            for l in range(lev):
                scaled[l] = filtered[l] / (1.0 + 4.0 * kappa[l])
        for copy in copies:
            copy.wait()
        edges = sides(1 + sweep)
        for l in range(lev):
            w, e, u, d = around(source, l, edges)
            target[l] = scaled[l] + coupling[l] * (w + e + u + d)


def solution(mesh):
    sectors, bands = mesh.shape["lon"], mesh.shape["lat"]

    def per_device(tracer, wind_east, wind_north, kappa, cutoff, partner):
        lev, rows, width = tracer.shape
        share = lev * (cutoff.shape[0] // 2) // sectors
        turns = SWEEPS + 1
        block = pltpu.VMEM((lev, rows, width), jnp.float32)
        vmem = pl.BlockSpec(memory_space=pltpu.VMEM)
        small = (cutoff.reshape(1, -1), partner.reshape(sectors, width), *tables(sectors, width))
        return pl.pallas_call(
            functools.partial(kernel, sectors, bands),
            out_shape=[jax.ShapeDtypeStruct(tracer.shape, jnp.float32)] * 2,
            in_specs=[pl.BlockSpec(memory_space=pltpu.HBM)] * 10,
            out_specs=[vmem] * 2,
            scratch_shapes=[
                block, block, block, block,
                *[pltpu.VMEM(a.shape, a.dtype) for a in small],
                pltpu.SemaphoreType.DMA((10,)),
                pltpu.VMEM((turns, 2, 8, width), jnp.float32),
                pltpu.VMEM((turns, 2, 8, width), jnp.float32),
                pltpu.VMEM((turns, 2 * lev, width), jnp.float32),
                pltpu.VMEM((turns, 4, 2 * lev, width), jnp.float32),
                pltpu.VMEM((sectors, share, width), jnp.float32),
                pltpu.VMEM((sectors, share, width), jnp.float32),
                pltpu.VMEM((sectors, share, width), jnp.float32),
                block, block, block, block,
                pltpu.SemaphoreType.DMA((turns, 6)),
                pltpu.SemaphoreType.DMA((turns, 6)),
                pltpu.SemaphoreType.DMA((sectors,)),
                pltpu.SemaphoreType.DMA((sectors,)),
                pltpu.SemaphoreType.DMA((sectors,)),
                pltpu.SemaphoreType.DMA((sectors,)),
            ],
            compiler_params=pltpu.CompilerParams(
                collective_id=0, has_side_effects=True, vmem_limit_bytes=60 * 1024 * 1024
            ),
        )(
            tracer, wind_east, wind_north, kappa, *small,
        )

    spec = P(None, "lat", "lon")
    return jax.shard_map(
        per_device, mesh=mesh, in_specs=(spec, spec, spec, spec, P(), P()), out_specs=(spec, spec),
        check_vma=False,
    )
```

```python
import functools
import math

import jax
import jax.numpy as jnp
import numpy as np
from jax import lax
from jax.experimental import pallas as pl
from jax.experimental.pallas import tpu as pltpu
from jax.sharding import PartitionSpec as P

KMAX = 512
SWEEPS = 4
COURANT = 0.4
HIGHEST = lax.Precision.HIGHEST


def tables(sectors, width):
    total = sectors * width
    half = sectors // 2
    m = np.arange(width)
    theta = 2.0 * np.pi * (np.outer(np.arange(half + 1), m) % total) / total
    kept = 2 * KMAX // sectors
    k2 = np.arange(kept) - kept // 2
    phase = 2.0 * np.pi * (np.outer(m, k2) % width) / width
    c, s = np.cos(phase), np.sin(phase)
    forward = np.block([[c, -s], [s, c]])
    inverse = np.block([[c.T, s.T], [-s.T, c.T]]) / total
    return [a.astype(np.float32) for a in (np.cos(theta), np.sin(theta), forward, inverse)]


def weighted(terms):
    total = None
    for factor, value in terms:
        if abs(factor) < 1e-12:
            continue
        part = value if abs(factor - 1.0) < 1e-12 else value * np.float32(factor)
        total = part if total is None else total + part
    return total


def kernel(
    sectors, bands,
    tracer_h, wind_east_h, wind_north_h, kappa_h, cutoff_h, partner_h, tw_cos_h, tw_sin_h, fwd_h, inv_h,
    filtered, balanced,
    tracer, wind_east, wind_north, kappa, cutoff, partner, tw_cos, tw_sin, fwd, inv, load_s,
    col_send, col_recv, edge_send, edge_recv, spread, send_b, recv_b, coupling, scaled, ping, pong,
    halo_ss, halo_rs, a_ss, a_rs, b_ss, b_rs,
):
    lev, rows, width = tracer.shape
    pole = cutoff.shape[1] // 2
    share = lev * pole // sectors
    slices = sectors // lev
    half = sectors // 2
    groups = lev * rows // 8
    per = rows // 8
    lat = lax.axis_index("lat")
    lon = lax.axis_index("lon")

    def sector(offset):
        return lax.rem(lon + (offset % sectors), sectors)

    def band(offset):
        return lax.rem(lat + (offset % bands), bands)

    held = (tracer_h, partner_h, wind_east_h, wind_north_h, kappa_h, cutoff_h, tw_cos_h, tw_sin_h, fwd_h, inv_h)
    near = (tracer, partner, wind_east, wind_north, kappa, cutoff, tw_cos, tw_sin, fwd, inv)
    loads = [pltpu.make_async_copy(h, v, load_s.at[i]) for i, (h, v) in enumerate(zip(held, near))]
    for load in loads:
        load.start()

    barrier = pltpu.get_barrier_semaphore()
    for t in range(1, sectors):
        pl.semaphore_signal(barrier, inc=1, device_id=(lat, sector(t)), device_id_type=pl.DeviceIdType.MESH)
    beside = (1,) if bands == 2 else (1, -1)
    for t in beside:
        pl.semaphore_signal(barrier, inc=1, device_id=(band(t), lon), device_id_type=pl.DeviceIdType.MESH)
    pl.semaphore_wait(barrier, sectors - 1 + len(beside))

    loads[0].wait()
    loads[1].wait()
    lane2 = lax.broadcasted_iota(jnp.int32, (rows, width), 1)
    row2 = lax.broadcasted_iota(jnp.int32, (rows, width), 0)
    diagonal = lax.broadcasted_iota(jnp.int32, (groups, 8, width), 0) == lax.broadcasted_iota(
        jnp.int32, (groups, 8, width), 2
    )
    reach = partner[pl.ds(lon, 1), :] - sector(half) * width
    reach = jnp.where(reach < 0, reach + sectors * width, reach)
    pick = jnp.where(
        lax.broadcasted_iota(jnp.int32, (2 * width, width), 0) == reach, 1.0, 0.0
    ).astype(jnp.bfloat16)
    lane8 = lax.broadcasted_iota(jnp.int32, (8, width), 1)
    row8 = lax.broadcasted_iota(jnp.int32, (8, width), 0)
    inner = lax.rem(lane8, per)
    level_of = lax.broadcasted_iota(jnp.int32, (lev, width), 0) * per
    place = lax.broadcasted_iota(jnp.int32, (lev, width), 1)
    head, tail = place == level_of, place == level_of + per - 1

    def column(field, at):
        whole = field[...].reshape(groups, 8, width)
        return jnp.sum(jnp.where(diagonal, whole[:, :, at : at + 1], 0.0), axis=0)

    def border(field, depth):
        return jnp.concatenate(
            [field[l, depth : depth + 1, :] for l in range(lev)]
            + [field[l, rows - 1 - depth : rows - depth, :] for l in range(lev)],
            axis=0,
        )

    def post(turn, edge, first_column, last_column):
        edge_send[turn] = edge
        col_send[turn, 0] = last_column
        col_send[turn, 1] = first_column
        plan = [
            (edge_send.at[turn], edge_recv.at[turn, 0], (lat, sector(-half))),
            (edge_send.at[turn], edge_recv.at[turn, 1], (lat, sector(-half - 1))),
            (edge_send.at[turn], edge_recv.at[turn, 2], (band(1), lon)),
            (col_send.at[turn, 0], col_recv.at[turn, 0], (lat, sector(1))),
            (col_send.at[turn, 1], col_recv.at[turn, 1], (lat, sector(-1))),
        ]
        if bands != 2:
            plan.append((edge_send.at[turn], edge_recv.at[turn, 3], (band(-1), lon)))
        copies = []
        for i, (src, dst, device) in enumerate(plan):
            copy = pltpu.make_async_remote_copy(
                src_ref=src, dst_ref=dst, send_sem=halo_ss.at[turn, i], recv_sem=halo_rs.at[turn, i],
                device_id=device, device_id_type=pl.DeviceIdType.MESH,
            )
            copy.start()
            copies.append(copy)
        return copies

    def outer(turn):
        x = jnp.concatenate([edge_recv[turn, 0], edge_recv[turn, 1]], axis=1)
        high = x.astype(jnp.bfloat16).astype(jnp.float32)
        rest = x - high
        middle = rest.astype(jnp.bfloat16).astype(jnp.float32)
        parts = jnp.concatenate([high, middle, rest - middle], axis=0).astype(jnp.bfloat16)
        found = jnp.dot(parts, pick, preferred_element_type=jnp.float32)
        n = 2 * lev
        across = found[:n] + found[n : 2 * n] + found[2 * n :]
        top = jnp.where(lat == 0, across[:lev], edge_recv[turn, 2, lev:])
        bottom = jnp.where(lat == bands - 1, across[lev:], edge_recv[turn, 2 if bands == 2 else 3, :lev])
        return top, bottom

    def sides(turn, top, bottom):
        west = jnp.sum(jnp.where(diagonal, col_recv[turn, 0][None], 0.0), axis=2, keepdims=True)
        east = jnp.sum(jnp.where(diagonal, col_recv[turn, 1][None], 0.0), axis=2, keepdims=True)
        return top, bottom, west, east

    def along(packed, top, bottom, at):
        above = jnp.sum(jnp.where(head, top[:, at : at + 1], 0.0), axis=0, keepdims=True)
        below = jnp.sum(jnp.where(tail, bottom[:, at : at + 1], 0.0), axis=0, keepdims=True)
        up, down = pltpu.roll(packed, 1, 0), pltpu.roll(packed, 7, 0)
        up = jnp.where(row8 == 0, jnp.where(inner == 0, above, pltpu.roll(up, 1, 1)), up)
        down = jnp.where(row8 == 7, jnp.where(inner == per - 1, below, pltpu.roll(down, width - 1, 1)), down)
        return up + down

    def ends(packed):
        return jnp.concatenate(
            [
                jnp.sum(jnp.where(head, packed[0:1], 0.0), axis=1, keepdims=True),
                jnp.sum(jnp.where(tail, packed[7:8], 0.0), axis=1, keepdims=True),
            ],
            axis=0,
        )

    def around(field, l, edges):
        top, bottom, west, east = edges
        x = field[l]
        w = jnp.broadcast_to(west[per * l : per * (l + 1)], (per, 8, width)).reshape(rows, width)
        e = jnp.broadcast_to(east[per * l : per * (l + 1)], (per, 8, width)).reshape(rows, width)
        return (
            jnp.where(lane2 == 0, w, pltpu.roll(x, 1, 1)),
            jnp.where(lane2 == width - 1, e, pltpu.roll(x, width - 1, 1)),
            jnp.where(row2 == 0, top[l : l + 1], pltpu.roll(x, 1, 0)),
            jnp.where(row2 == rows - 1, bottom[l : l + 1], pltpu.roll(x, rows - 1, 0)),
        )

    copies = post(0, border(tracer, 0), column(tracer, 0), column(tracer, width - 1))
    for load in loads[2:]:
        load.wait()
    for l in range(lev):
        coupling[l] = kappa[l] / (1.0 + 4.0 * kappa[l])
    for copy in copies:
        copy.wait()
    edges = sides(0, *outer(0))
    for l in range(lev):
        w, e, u, d = around(tracer, l, edges)
        filtered[l] = tracer[l] - COURANT * 0.5 * (wind_east[l] * (e - w) + wind_north[l] * (d - u))

    base = jnp.where(lat == bands - 1, rows - pole, 0)

    def part(device):
        return lax.div(device, slices), pl.ds(pl.multiple_of(base + lax.rem(device, slices) * share, 8), share)

    copies = []
    for t in range(1, sectors):
        level, span = part(sector(t))
        copy = pltpu.make_async_remote_copy(
            src_ref=filtered.at[level, span, :], dst_ref=spread.at[lon],
            send_sem=a_ss.at[t], recv_sem=a_rs.at[t],
            device_id=(lat, sector(t)), device_id_type=pl.DeviceIdType.MESH,
        )
        copy.start()
        copies.append(copy)
    level, span = part(lon)
    spread[lon] = filtered[level, span, :]

    first = jnp.where(lat == bands - 1, pole, 0) + lax.rem(lon, slices) * share
    spot = lax.broadcasted_iota(jnp.int32, (share, 2 * pole), 0) + first
    limit = jnp.sum(
        jnp.where(
            lax.broadcasted_iota(jnp.int32, (share, 2 * pole), 1) == spot,
            cutoff[...].astype(jnp.float32), 0.0,
        ),
        axis=1, keepdims=True,
    )
    kept = 2 * KMAX // sectors
    slot = lax.broadcasted_iota(jnp.int32, (share, 2 * kept), 1)
    wave = sectors * (jnp.where(slot < kept, slot, slot - kept) - kept // 2)
    for copy in copies:
        copy.wait()

    def circle(d, k):
        angle = 2.0 * math.pi * ((d * k) % sectors) / sectors
        return math.cos(angle), math.sin(angle)

    even = [spread[0]] + [spread[d] + spread[sectors - d] for d in range(1, half)] + [spread[half]]
    odd = [None] + [spread[d] - spread[sectors - d] for d in range(1, half)]
    blocks = []
    for k in range(half + 1):
        c, s = tw_cos[k : k + 1, :], tw_sin[k : k + 1, :]
        re = weighted([(circle(d, k)[0], even[d]) for d in range(half + 1)])
        im = weighted([(-circle(d, k)[1], odd[d]) for d in range(1, half)])
        if im is None:
            blocks.append(jnp.concatenate([re * c, -(re * s)], axis=1))
        else:
            blocks.append(jnp.concatenate([re * c + im * s, im * c - re * s], axis=1))
    spectrum = jnp.dot(
        jnp.concatenate(blocks, axis=0), fwd[...], precision=HIGHEST, preferred_element_type=jnp.float32
    )
    keep = jnp.concatenate(
        [jnp.where(jnp.abs(wave + k).astype(jnp.float32) <= limit, 1.0, 0.0) for k in range(half + 1)], axis=0
    )
    back = jnp.dot(
        jnp.where(keep > 0.0, spectrum, 0.0), inv[...], precision=HIGHEST, preferred_element_type=jnp.float32
    )
    real, imag = [], []
    for k in range(half + 1):
        c, s = tw_cos[k : k + 1, :], tw_sin[k : k + 1, :]
        zr = back[k * share : (k + 1) * share, :width]
        zi = back[k * share : (k + 1) * share, width:]
        twice = 1.0 if k in (0, half) else 2.0
        real.append((zr * c - zi * s) * twice)
        imag.append((zr * s + zi * c) * twice)
    for d in range(half + 1):
        p = weighted([(circle(d, k)[0], real[k]) for k in range(half + 1)])
        q = weighted([(circle(d, k)[1], imag[k]) for k in range(1, half)])
        if q is None:
            send_b[d] = p
        else:
            send_b[d] = p - q
            send_b[sectors - d] = p + q

    copies = []
    for t in range(1, sectors):
        copy = pltpu.make_async_remote_copy(
            src_ref=send_b.at[sector(t)], dst_ref=recv_b.at[lon],
            send_sem=b_ss.at[t], recv_sem=b_rs.at[t],
            device_id=(lat, sector(t)), device_id_type=pl.DeviceIdType.MESH,
        )
        copy.start()
        copies.append(copy)
    recv_b[lon] = send_b[lon]
    for copy in copies:
        copy.wait()

    def restore(start):
        for l in range(lev):
            for q in range(slices):
                filtered[l, start + q * share : start + (q + 1) * share, :] = recv_b[l * slices + q]

    @pl.when(lat == 0)
    def _():
        restore(0)

    @pl.when(lat == bands - 1)
    def _():
        restore(rows - pole)

    edge, first_column, last_column = border(filtered, 0), column(filtered, 0), column(filtered, width - 1)
    copies = post(1, edge, first_column, last_column)
    for l in range(lev):
        scaled[l] = filtered[l] / (1.0 + 4.0 * kappa[l])
    fixed = [(border(a, 0), column(a, 0), column(a, width - 1)) for a in (scaled, coupling)]
    chain = [filtered, ping, pong, ping, balanced]
    for sweep in range(SWEEPS):
        turn, source, target = 1 + sweep, chain[sweep], chain[sweep + 1]
        if sweep < SWEEPS - 1:
            second, second_first, second_last = border(source, 1), column(source, 1), column(source, width - 2)
        for copy in copies:
            copy.wait()
        top, bottom = outer(turn)
        if sweep < SWEEPS - 1:
            west, east = col_recv[turn, 0], col_recv[turn, 1]
            around_edge = (
                jnp.where(lane8 == 0, ends(west), pltpu.roll(edge, 1, 1))
                + jnp.where(lane8 == width - 1, ends(east), pltpu.roll(edge, width - 1, 1))
                + jnp.concatenate([top, bottom], axis=0)
                + second
            )
            around_first = west + second_first + along(first_column, top, bottom, 0)
            around_last = east + second_last + along(last_column, top, bottom, width - 1)
            edge, first_column, last_column = [
                a + b * c for a, b, c in zip(*fixed, (around_edge, around_first, around_last))
            ]
            copies = post(turn + 1, edge, first_column, last_column)
        edges = sides(turn, top, bottom)
        for l in range(lev):
            w, e, u, d = around(source, l, edges)
            target[l] = scaled[l] + coupling[l] * (w + e + u + d)


def solution(mesh):
    sectors, bands = mesh.shape["lon"], mesh.shape["lat"]

    def per_device(tracer, wind_east, wind_north, kappa, cutoff, partner):
        lev, rows, width = tracer.shape
        share = lev * (cutoff.shape[0] // 2) // sectors
        turns = SWEEPS + 1
        block = pltpu.VMEM((lev, rows, width), jnp.float32)
        vmem = pl.BlockSpec(memory_space=pltpu.VMEM)
        small = (cutoff.reshape(1, -1), partner.reshape(sectors, width), *tables(sectors, width))
        return pl.pallas_call(
            functools.partial(kernel, sectors, bands),
            out_shape=[jax.ShapeDtypeStruct(tracer.shape, jnp.float32)] * 2,
            in_specs=[pl.BlockSpec(memory_space=pltpu.HBM)] * 10,
            out_specs=[vmem] * 2,
            scratch_shapes=[
                block, block, block, block,
                *[pltpu.VMEM(a.shape, a.dtype) for a in small],
                pltpu.SemaphoreType.DMA((10,)),
                pltpu.VMEM((turns, 2, 8, width), jnp.float32),
                pltpu.VMEM((turns, 2, 8, width), jnp.float32),
                pltpu.VMEM((turns, 2 * lev, width), jnp.float32),
                pltpu.VMEM((turns, 4, 2 * lev, width), jnp.float32),
                pltpu.VMEM((sectors, share, width), jnp.float32),
                pltpu.VMEM((sectors, share, width), jnp.float32),
                pltpu.VMEM((sectors, share, width), jnp.float32),
                block, block, block, block,
                pltpu.SemaphoreType.DMA((turns, 6)),
                pltpu.SemaphoreType.DMA((turns, 6)),
                pltpu.SemaphoreType.DMA((sectors,)),
                pltpu.SemaphoreType.DMA((sectors,)),
                pltpu.SemaphoreType.DMA((sectors,)),
                pltpu.SemaphoreType.DMA((sectors,)),
            ],
            compiler_params=pltpu.CompilerParams(
                collective_id=0, has_side_effects=True, vmem_limit_bytes=32 * 1024 * 1024
            ),
        )(
            *[pltpu.with_memory_space_constraint(jnp.asarray(a), pltpu.HBM) for a in (tracer, wind_east, wind_north, kappa, *small)]
        )

    spec = P(None, "lat", "lon")
    return jax.shard_map(
        per_device, mesh=mesh, in_specs=(spec, spec, spec, spec, P(), P()), out_specs=(spec, spec),
        check_vma=False,
    )
```

```python
import functools
import math

import jax
import jax.numpy as jnp
import numpy as np
from jax import lax
from jax.experimental import pallas as pl
from jax.experimental.pallas import tpu as pltpu
from jax.sharding import PartitionSpec as P

KMAX = 512
SWEEPS = 4
COURANT = 0.4
HIGHEST = lax.Precision.HIGHEST


def tables(sectors, width):
    total = sectors * width
    half = sectors // 2
    m = np.arange(width)
    theta = 2.0 * np.pi * (np.outer(np.arange(half + 1), m) % total) / total
    kept = 2 * KMAX // sectors
    k2 = np.arange(kept) - kept // 2
    phase = 2.0 * np.pi * (np.outer(m, k2) % width) / width
    c, s = np.cos(phase), np.sin(phase)
    forward = np.block([[c, -s], [s, c]])
    inverse = np.block([[c.T, s.T], [-s.T, c.T]]) / total
    return [a.astype(np.float32) for a in (np.cos(theta), np.sin(theta), forward, inverse)]


def weighted(terms):
    total = None
    for factor, value in terms:
        if abs(factor) < 1e-12:
            continue
        part = value if abs(factor - 1.0) < 1e-12 else value * np.float32(factor)
        total = part if total is None else total + part
    return total


def kernel(
    sectors, bands,
    tracer_h, wind_east_h, wind_north_h, kappa_h, cutoff_h, partner_h, tw_cos_h, tw_sin_h, fwd_h, inv_h,
    filtered, balanced,
    tracer, wind_east, wind_north, kappa, cutoff, partner, tw_cos, tw_sin, fwd, inv, load_s,
    col_send, col_recv, edge_send, edge_recv, stage, spread, send_b, recv_b, coupling, scaled, ping, pong,
    halo_ss, halo_rs, a_ss, a_rs, b_ss, b_rs,
):
    lev, rows, width = tracer.shape
    pole = cutoff.shape[1] // 2
    share = lev * pole // sectors
    slices = sectors // lev
    half = sectors // 2
    groups = lev * rows // 8
    per = rows // 8
    lat = lax.axis_index("lat")
    lon = lax.axis_index("lon")

    def sector(offset):
        return lax.rem(lon + (offset % sectors), sectors)

    def band(offset):
        return lax.rem(lat + (offset % bands), bands)

    held = (tracer_h, partner_h, wind_east_h, wind_north_h, kappa_h, cutoff_h, tw_cos_h, tw_sin_h, fwd_h, inv_h)
    near = (tracer, partner, wind_east, wind_north, kappa, cutoff, tw_cos, tw_sin, fwd, inv)
    loads = [pltpu.make_async_copy(h, v, load_s.at[i]) for i, (h, v) in enumerate(zip(held, near))]
    for load in loads:
        load.start()

    barrier = pltpu.get_barrier_semaphore()
    for t in range(1, sectors):
        pl.semaphore_signal(barrier, inc=1, device_id=(lat, sector(t)), device_id_type=pl.DeviceIdType.MESH)
    beside = (1,) if bands == 2 else (1, -1)
    for t in beside:
        pl.semaphore_signal(barrier, inc=1, device_id=(band(t), lon), device_id_type=pl.DeviceIdType.MESH)
    pl.semaphore_wait(barrier, sectors - 1 + len(beside))

    loads[0].wait()
    loads[1].wait()
    lane2 = lax.broadcasted_iota(jnp.int32, (rows, width), 1)
    row2 = lax.broadcasted_iota(jnp.int32, (rows, width), 0)
    diagonal = lax.broadcasted_iota(jnp.int32, (groups, 8, width), 0) == lax.broadcasted_iota(
        jnp.int32, (groups, 8, width), 2
    )
    reach = partner[pl.ds(lon, 1), :] - sector(half) * width
    reach = jnp.where(reach < 0, reach + sectors * width, reach)
    pick = jnp.where(
        lax.broadcasted_iota(jnp.int32, (2 * width, width), 0) == reach, 1.0, 0.0
    ).astype(jnp.bfloat16)
    lane8 = lax.broadcasted_iota(jnp.int32, (8, width), 1)
    row8 = lax.broadcasted_iota(jnp.int32, (8, width), 0)
    inner = lax.rem(lane8, per)
    level_of = lax.broadcasted_iota(jnp.int32, (lev, width), 0) * per
    place = lax.broadcasted_iota(jnp.int32, (lev, width), 1)
    head, tail = place == level_of, place == level_of + per - 1

    def column(field, at):
        whole = field[...].reshape(groups, 8, width)
        return jnp.sum(jnp.where(diagonal, whole[:, :, at : at + 1], 0.0), axis=0)

    def border(field, depth):
        return jnp.concatenate(
            [field[l, depth : depth + 1, :] for l in range(lev)]
            + [field[l, rows - 1 - depth : rows - depth, :] for l in range(lev)],
            axis=0,
        )

    def post(turn, edge, first_column, last_column):
        edge_send[turn] = edge
        col_send[turn, 0] = last_column
        col_send[turn, 1] = first_column
        plan = [
            (edge_send.at[turn], edge_recv.at[turn, 0], (lat, sector(-half))),
            (edge_send.at[turn], edge_recv.at[turn, 1], (lat, sector(-half - 1))),
            (edge_send.at[turn], edge_recv.at[turn, 2], (band(1), lon)),
            (col_send.at[turn, 0], col_recv.at[turn, 0], (lat, sector(1))),
            (col_send.at[turn, 1], col_recv.at[turn, 1], (lat, sector(-1))),
        ]
        if bands != 2:
            plan.append((edge_send.at[turn], edge_recv.at[turn, 3], (band(-1), lon)))
        copies = []
        for i, (src, dst, device) in enumerate(plan):
            copy = pltpu.make_async_remote_copy(
                src_ref=src, dst_ref=dst, send_sem=halo_ss.at[turn, i], recv_sem=halo_rs.at[turn, i],
                device_id=device, device_id_type=pl.DeviceIdType.MESH,
            )
            copy.start()
            copies.append(copy)
        return copies

    def outer(turn):
        x = jnp.concatenate([edge_recv[turn, 0], edge_recv[turn, 1]], axis=1)
        high = x.astype(jnp.bfloat16).astype(jnp.float32)
        rest = x - high
        middle = rest.astype(jnp.bfloat16).astype(jnp.float32)
        parts = jnp.concatenate([high, middle, rest - middle], axis=0).astype(jnp.bfloat16)
        found = jnp.dot(parts, pick, preferred_element_type=jnp.float32)
        n = 2 * lev
        across = found[:n] + found[n : 2 * n] + found[2 * n :]
        top = jnp.where(lat == 0, across[:lev], edge_recv[turn, 2, lev:])
        bottom = jnp.where(lat == bands - 1, across[lev:], edge_recv[turn, 2 if bands == 2 else 3, :lev])
        return top, bottom

    def sides(turn, top, bottom):
        west = jnp.sum(jnp.where(diagonal, col_recv[turn, 0][None], 0.0), axis=2, keepdims=True)
        east = jnp.sum(jnp.where(diagonal, col_recv[turn, 1][None], 0.0), axis=2, keepdims=True)
        return top, bottom, west, east

    def along(packed, top, bottom, at):
        above = jnp.sum(jnp.where(head, top[:, at : at + 1], 0.0), axis=0, keepdims=True)
        below = jnp.sum(jnp.where(tail, bottom[:, at : at + 1], 0.0), axis=0, keepdims=True)
        up, down = pltpu.roll(packed, 1, 0), pltpu.roll(packed, 7, 0)
        up = jnp.where(row8 == 0, jnp.where(inner == 0, above, pltpu.roll(up, 1, 1)), up)
        down = jnp.where(row8 == 7, jnp.where(inner == per - 1, below, pltpu.roll(down, width - 1, 1)), down)
        return up + down

    def ends(packed):
        return jnp.concatenate(
            [
                jnp.sum(jnp.where(head, packed[0:1], 0.0), axis=1, keepdims=True),
                jnp.sum(jnp.where(tail, packed[7:8], 0.0), axis=1, keepdims=True),
            ],
            axis=0,
        )

    def around(field, l, edges):
        top, bottom, west, east = edges
        x = field[l]
        w = jnp.broadcast_to(west[per * l : per * (l + 1)], (per, 8, width)).reshape(rows, width)
        e = jnp.broadcast_to(east[per * l : per * (l + 1)], (per, 8, width)).reshape(rows, width)
        return (
            jnp.where(lane2 == 0, w, pltpu.roll(x, 1, 1)),
            jnp.where(lane2 == width - 1, e, pltpu.roll(x, width - 1, 1)),
            jnp.where(row2 == 0, top[l : l + 1], pltpu.roll(x, 1, 0)),
            jnp.where(row2 == rows - 1, bottom[l : l + 1], pltpu.roll(x, rows - 1, 0)),
        )

    copies = post(0, border(tracer, 0), column(tracer, 0), column(tracer, width - 1))
    for load in loads[2:]:
        load.wait()
    for l in range(lev):
        inverse = 1.0 / (1.0 + 4.0 * kappa[l])
        scaled[l] = inverse
        coupling[l] = kappa[l] * inverse
    last = lat == bands - 1
    base = pl.multiple_of(jnp.where(last, rows - pole, 0), 8)
    before = jnp.where(last, rows - pole - 1, 0)
    after = jnp.where(last, rows - 1, pole)
    offset = jnp.where(last, (rows - pole) // 8, 0)
    shape = (pole // 8, 8, width)
    lane_p = lax.broadcasted_iota(jnp.int32, (pole, width), 1)
    row_p = lax.broadcasted_iota(jnp.int32, (pole, width), 0)
    for copy in copies:
        copy.wait()
    top, bottom = outer(0)

    def spoke(packed, l):
        mine = lax.broadcasted_iota(jnp.int32, shape, 0) + (per * l + offset) == lax.broadcasted_iota(
            jnp.int32, shape, 2
        )
        value = jnp.sum(jnp.where(mine, packed[None], 0.0), axis=2, keepdims=True)
        return jnp.broadcast_to(value, shape).reshape(pole, width)

    def to_share(l, q):
        device = l * slices + q
        return pltpu.make_async_remote_copy(
            src_ref=stage.at[l, pl.ds(q * share, share), :], dst_ref=spread.at[lon],
            send_sem=a_ss.at[device], recv_sem=a_rs.at[lon],
            device_id=(lat, device), device_id_type=pl.DeviceIdType.MESH,
        )

    for l in range(lev):
        x = tracer[l, pl.ds(base, pole), :]
        w = jnp.where(lane_p == 0, spoke(col_recv[0, 0], l), pltpu.roll(x, 1, 1))
        e = jnp.where(lane_p == width - 1, spoke(col_recv[0, 1], l), pltpu.roll(x, width - 1, 1))
        above = jnp.where(last, tracer[l, pl.ds(before, 1), :], top[l : l + 1])
        below = jnp.where(last, bottom[l : l + 1], tracer[l, pl.ds(after, 1), :])
        u = jnp.where(row_p == 0, above, pltpu.roll(x, 1, 0))
        d = jnp.where(row_p == pole - 1, below, pltpu.roll(x, pole - 1, 0))
        stage[l] = x - COURANT * 0.5 * (
            wind_east[l, pl.ds(base, pole), :] * (e - w) + wind_north[l, pl.ds(base, pole), :] * (d - u)
        )
        for q in range(slices):
            @pl.when(lon != l * slices + q)
            def _(l=l, q=q):
                to_share(l, q).start()

            @pl.when(lon == l * slices + q)
            def _(l=l, q=q):
                spread[l * slices + q] = stage[l, q * share : (q + 1) * share, :]

    edges = sides(0, top, bottom)
    for l in range(lev):
        w, e, u, d = around(tracer, l, edges)
        filtered[l] = tracer[l] - COURANT * 0.5 * (wind_east[l] * (e - w) + wind_north[l] * (d - u))
    fixed = [(border(a, 0), column(a, 0), column(a, width - 1)) for a in (scaled, coupling)]

    first = jnp.where(lat == bands - 1, pole, 0) + lax.rem(lon, slices) * share
    spot = lax.broadcasted_iota(jnp.int32, (share, 2 * pole), 0) + first
    limit = jnp.sum(
        jnp.where(
            lax.broadcasted_iota(jnp.int32, (share, 2 * pole), 1) == spot,
            cutoff[...].astype(jnp.float32), 0.0,
        ),
        axis=1, keepdims=True,
    )
    kept = 2 * KMAX // sectors
    slot = lax.broadcasted_iota(jnp.int32, (share, 2 * kept), 1)
    wave = sectors * (jnp.where(slot < kept, slot, slot - kept) - kept // 2)
    for device in range(sectors):
        @pl.when(lon != device)
        def _(device=device):
            pltpu.make_async_remote_copy(
                src_ref=stage.at[device // slices, pl.ds(device % slices * share, share), :],
                dst_ref=spread.at[device], send_sem=a_ss.at[device], recv_sem=a_rs.at[device],
                device_id=(lat, device), device_id_type=pl.DeviceIdType.MESH,
            ).wait()

    def circle(d, k):
        angle = 2.0 * math.pi * ((d * k) % sectors) / sectors
        return math.cos(angle), math.sin(angle)

    even = [spread[0]] + [spread[d] + spread[sectors - d] for d in range(1, half)] + [spread[half]]
    odd = [None] + [spread[d] - spread[sectors - d] for d in range(1, half)]
    blocks = []
    for k in range(half + 1):
        c, s = tw_cos[k : k + 1, :], tw_sin[k : k + 1, :]
        re = weighted([(circle(d, k)[0], even[d]) for d in range(half + 1)])
        im = weighted([(-circle(d, k)[1], odd[d]) for d in range(1, half)])
        if im is None:
            blocks.append(jnp.concatenate([re * c, -(re * s)], axis=1))
        else:
            blocks.append(jnp.concatenate([re * c + im * s, im * c - re * s], axis=1))
    spectrum = jnp.dot(
        jnp.concatenate(blocks, axis=0), fwd[...], precision=HIGHEST, preferred_element_type=jnp.float32
    )
    keep = jnp.concatenate(
        [jnp.where(jnp.abs(wave + k).astype(jnp.float32) <= limit, 1.0, 0.0) for k in range(half + 1)], axis=0
    )
    back = jnp.dot(
        jnp.where(keep > 0.0, spectrum, 0.0), inv[...], precision=HIGHEST, preferred_element_type=jnp.float32
    )
    real, imag = [], []
    for k in range(half + 1):
        c, s = tw_cos[k : k + 1, :], tw_sin[k : k + 1, :]
        zr = back[k * share : (k + 1) * share, :width]
        zi = back[k * share : (k + 1) * share, width:]
        twice = 1.0 if k in (0, half) else 2.0
        real.append((zr * c - zi * s) * twice)
        imag.append((zr * s + zi * c) * twice)
    for d in range(half + 1):
        p = weighted([(circle(d, k)[0], real[k]) for k in range(half + 1)])
        q = weighted([(circle(d, k)[1], imag[k]) for k in range(1, half)])
        if q is None:
            send_b[d] = p
        else:
            send_b[d] = p - q
            send_b[sectors - d] = p + q

    copies = []
    for t in range(1, sectors):
        copy = pltpu.make_async_remote_copy(
            src_ref=send_b.at[sector(t)], dst_ref=recv_b.at[lon],
            send_sem=b_ss.at[t], recv_sem=b_rs.at[t],
            device_id=(lat, sector(t)), device_id_type=pl.DeviceIdType.MESH,
        )
        copy.start()
        copies.append(copy)
    recv_b[lon] = send_b[lon]
    plain = border(filtered, 0), column(filtered, 0), column(filtered, width - 1)
    polar = (lat == 0) | last
    for copy in copies:
        copy.wait()

    cells = recv_b[...].reshape(lev * pole // 8, 8, width)
    order = lax.broadcasted_iota(jnp.int32, cells.shape, 0)
    order = lax.div(order, pole // 8) * per + offset + lax.rem(order, pole // 8)
    mine = order == lax.broadcasted_iota(jnp.int32, cells.shape, 2)
    step = lax.rem(lane8, per) - offset
    fresh = (step >= 0) & (step < pole // 8) & polar

    def renewed(old, at):
        return jnp.where(fresh, jnp.sum(jnp.where(mine, cells[:, :, at : at + 1], 0.0), axis=0), old)

    rim = jnp.concatenate(
        [recv_b[l * slices, 0:1, :] for l in range(lev)]
        + [recv_b[l * slices + slices - 1, share - 1 : share, :] for l in range(lev)],
        axis=0,
    )
    edge = jnp.where(((row8 < lev) & (lat == 0)) | ((row8 >= lev) & last), rim, plain[0])
    first_column, last_column = renewed(plain[1], 0), renewed(plain[2], width - 1)
    copies = post(1, edge, first_column, last_column)
    fixed[0] = tuple(a * b for a, b in zip(fixed[0], (edge, first_column, last_column)))

    def restore(start):
        for l in range(lev):
            for q in range(slices):
                filtered[l, start + q * share : start + (q + 1) * share, :] = recv_b[l * slices + q]

    @pl.when(lat == 0)
    def _():
        restore(0)

    @pl.when(lat == bands - 1)
    def _():
        restore(rows - pole)

    for l in range(lev):
        scaled[l] = filtered[l] * scaled[l]
    chain = [filtered, ping, pong, ping, balanced]
    for sweep in range(SWEEPS):
        turn, source, target = 1 + sweep, chain[sweep], chain[sweep + 1]
        if sweep < SWEEPS - 1:
            second, second_first, second_last = border(source, 1), column(source, 1), column(source, width - 2)
        for copy in copies:
            copy.wait()
        top, bottom = outer(turn)
        if sweep < SWEEPS - 1:
            west, east = col_recv[turn, 0], col_recv[turn, 1]
            around_edge = (
                jnp.where(lane8 == 0, ends(west), pltpu.roll(edge, 1, 1))
                + jnp.where(lane8 == width - 1, ends(east), pltpu.roll(edge, width - 1, 1))
                + jnp.concatenate([top, bottom], axis=0)
                + second
            )
            around_first = west + second_first + along(first_column, top, bottom, 0)
            around_last = east + second_last + along(last_column, top, bottom, width - 1)
            edge, first_column, last_column = [
                a + b * c for a, b, c in zip(*fixed, (around_edge, around_first, around_last))
            ]
            copies = post(turn + 1, edge, first_column, last_column)
        edges = sides(turn, top, bottom)
        for l in range(lev):
            w, e, u, d = around(source, l, edges)
            target[l] = scaled[l] + coupling[l] * (w + e + u + d)


def solution(mesh):
    sectors, bands = mesh.shape["lon"], mesh.shape["lat"]

    def per_device(tracer, wind_east, wind_north, kappa, cutoff, partner):
        lev, rows, width = tracer.shape
        share = lev * (cutoff.shape[0] // 2) // sectors
        turns = SWEEPS + 1
        block = pltpu.VMEM((lev, rows, width), jnp.float32)
        vmem = pl.BlockSpec(memory_space=pltpu.VMEM)
        small = (cutoff.reshape(1, -1), partner.reshape(sectors, width), *tables(sectors, width))
        return pl.pallas_call(
            functools.partial(kernel, sectors, bands),
            out_shape=[jax.ShapeDtypeStruct(tracer.shape, jnp.float32)] * 2,
            in_specs=[pl.BlockSpec(memory_space=pltpu.HBM)] * 10,
            out_specs=[vmem] * 2,
            scratch_shapes=[
                block, block, block, block,
                *[pltpu.VMEM(a.shape, a.dtype) for a in small],
                pltpu.SemaphoreType.DMA((10,)),
                pltpu.VMEM((turns, 2, 8, width), jnp.float32),
                pltpu.VMEM((turns, 2, 8, width), jnp.float32),
                pltpu.VMEM((turns, 2 * lev, width), jnp.float32),
                pltpu.VMEM((turns, 4, 2 * lev, width), jnp.float32),
                pltpu.VMEM((lev, cutoff.shape[0] // 2, width), jnp.float32),
                pltpu.VMEM((sectors, share, width), jnp.float32),
                pltpu.VMEM((sectors, share, width), jnp.float32),
                pltpu.VMEM((sectors, share, width), jnp.float32),
                block, block, block, block,
                pltpu.SemaphoreType.DMA((turns, 6)),
                pltpu.SemaphoreType.DMA((turns, 6)),
                pltpu.SemaphoreType.DMA((sectors,)),
                pltpu.SemaphoreType.DMA((sectors,)),
                pltpu.SemaphoreType.DMA((sectors,)),
                pltpu.SemaphoreType.DMA((sectors,)),
            ],
            compiler_params=pltpu.CompilerParams(
                collective_id=0, has_side_effects=True, vmem_limit_bytes=32 * 1024 * 1024
            ),
        )(
            *[pltpu.with_memory_space_constraint(jnp.asarray(a), pltpu.HBM) for a in (tracer, wind_east, wind_north, kappa, *small)]
        )

    spec = P(None, "lat", "lon")
    return jax.shard_map(
        per_device, mesh=mesh, in_specs=(spec, spec, spec, spec, P(), P()), out_specs=(spec, spec),
        check_vma=False,
    )
```

```python
import functools
import math

import jax
import jax.numpy as jnp
import numpy as np
from jax import lax
from jax.experimental import pallas as pl
from jax.experimental.pallas import tpu as pltpu
from jax.sharding import PartitionSpec as P

KMAX = 512
SWEEPS = 4
COURANT = 0.4
HIGHEST = lax.Precision.HIGHEST


def tables(sectors, width):
    total = sectors * width
    half = sectors // 2
    m = np.arange(width)
    theta = 2.0 * np.pi * (np.outer(np.arange(half + 1), m) % total) / total
    kept = 2 * KMAX // sectors
    k2 = np.arange(kept) - kept // 2
    phase = 2.0 * np.pi * (np.outer(m, k2) % width) / width
    c, s = np.cos(phase), np.sin(phase)
    forward = np.block([[c, -s], [s, c]])
    inverse = np.block([[c.T, s.T], [-s.T, c.T]]) / total
    return [a.astype(np.float32) for a in (np.cos(theta), np.sin(theta), forward, inverse)]


def weighted(terms):
    total = None
    for factor, value in terms:
        if abs(factor) < 1e-12:
            continue
        part = value if abs(factor - 1.0) < 1e-12 else value * np.float32(factor)
        total = part if total is None else total + part
    return total


def kernel(
    sectors, bands,
    tracer_h, wind_east_h, wind_north_h, kappa_h, cutoff_h, partner_h, tw_cos_h, tw_sin_h, fwd_h, inv_h,
    filtered, balanced,
    tracer, wind_east, wind_north, kappa, cutoff, partner, tw_cos, tw_sin, fwd, inv, load_s,
    col_send, col_recv, edge_send, edge_recv, stage, spread, send_b, recv_b, coupling, scaled, ping, pong,
    halo_ss, halo_rs, a_ss, a_rs, b_ss, b_rs,
):
    lev, rows, width = tracer.shape
    pole = cutoff.shape[1] // 2
    share = lev * pole // sectors
    slices = sectors // lev
    half = sectors // 2
    groups = lev * rows // 8
    per = rows // 8
    lat = lax.axis_index("lat")
    lon = lax.axis_index("lon")

    def sector(offset):
        return lax.rem(lon + (offset % sectors), sectors)

    def band(offset):
        return lax.rem(lat + (offset % bands), bands)

    held = (tracer_h, partner_h, wind_east_h, wind_north_h, kappa_h, cutoff_h, tw_cos_h, tw_sin_h, fwd_h, inv_h)
    near = (tracer, partner, wind_east, wind_north, kappa, cutoff, tw_cos, tw_sin, fwd, inv)
    loads = [pltpu.make_async_copy(h, v, load_s.at[i]) for i, (h, v) in enumerate(zip(held, near))]
    for load in loads:
        load.start()

    barrier = pltpu.get_barrier_semaphore()
    for t in range(1, sectors):
        pl.semaphore_signal(barrier, inc=1, device_id=(lat, sector(t)), device_id_type=pl.DeviceIdType.MESH)
    beside = (1,) if bands == 2 else (1, -1)
    for t in beside:
        pl.semaphore_signal(barrier, inc=1, device_id=(band(t), lon), device_id_type=pl.DeviceIdType.MESH)
    pl.semaphore_wait(barrier, sectors - 1 + len(beside))

    loads[0].wait()
    loads[1].wait()
    lane2 = lax.broadcasted_iota(jnp.int32, (rows, width), 1)
    row2 = lax.broadcasted_iota(jnp.int32, (rows, width), 0)
    diagonal = lax.broadcasted_iota(jnp.int32, (groups, 8, width), 0) == lax.broadcasted_iota(
        jnp.int32, (groups, 8, width), 2
    )
    reach = partner[pl.ds(lon, 1), :] - sector(half) * width
    reach = jnp.where(reach < 0, reach + sectors * width, reach)
    pick = jnp.where(
        lax.broadcasted_iota(jnp.int32, (2 * width, width), 0) == reach, 1.0, 0.0
    ).astype(jnp.bfloat16)
    lane8 = lax.broadcasted_iota(jnp.int32, (8, width), 1)
    row8 = lax.broadcasted_iota(jnp.int32, (8, width), 0)
    inner = lax.rem(lane8, per)
    level_of = lax.broadcasted_iota(jnp.int32, (lev, width), 0) * per
    place = lax.broadcasted_iota(jnp.int32, (lev, width), 1)
    head, tail = place == level_of, place == level_of + per - 1

    sent = []

    def column(field, at):
        whole = field[...].reshape(groups, 8, width)
        return jnp.sum(jnp.where(diagonal, whole[:, :, at : at + 1], 0.0), axis=0)

    def border(field, depth):
        return jnp.concatenate(
            [field[l, depth : depth + 1, :] for l in range(lev)]
            + [field[l, rows - 1 - depth : rows - depth, :] for l in range(lev)],
            axis=0,
        )

    def post(turn, edge, first_column, last_column):
        edge_send[turn] = edge
        col_send[turn, 0] = last_column
        col_send[turn, 1] = first_column
        plan = [
            (edge_send.at[turn], edge_recv.at[turn, 0], (lat, sector(-half))),
            (edge_send.at[turn], edge_recv.at[turn, 1], (lat, sector(-half - 1))),
            (edge_send.at[turn], edge_recv.at[turn, 2], (band(1), lon)),
            (col_send.at[turn, 0], col_recv.at[turn, 0], (lat, sector(1))),
            (col_send.at[turn, 1], col_recv.at[turn, 1], (lat, sector(-1))),
        ]
        if bands != 2:
            plan.append((edge_send.at[turn], edge_recv.at[turn, 3], (band(-1), lon)))
        copies = []
        for i, (src, dst, device) in enumerate(plan):
            copy = pltpu.make_async_remote_copy(
                src_ref=src, dst_ref=dst, send_sem=halo_ss.at[turn, i], recv_sem=halo_rs.at[turn, i],
                device_id=device, device_id_type=pl.DeviceIdType.MESH,
            )
            copy.start()
            copies.append(copy)
        sent.extend(copies)
        return copies

    def outer(turn):
        x = jnp.concatenate([edge_recv[turn, 0], edge_recv[turn, 1]], axis=1)
        high = x.astype(jnp.bfloat16).astype(jnp.float32)
        rest = x - high
        middle = rest.astype(jnp.bfloat16).astype(jnp.float32)
        parts = jnp.concatenate([high, middle, rest - middle], axis=0).astype(jnp.bfloat16)
        found = jnp.dot(parts, pick, preferred_element_type=jnp.float32)
        n = 2 * lev
        across = found[:n] + found[n : 2 * n] + found[2 * n :]
        top = jnp.where(lat == 0, across[:lev], edge_recv[turn, 2, lev:])
        bottom = jnp.where(lat == bands - 1, across[lev:], edge_recv[turn, 2 if bands == 2 else 3, :lev])
        return top, bottom

    def sides(turn, top, bottom):
        west = jnp.sum(jnp.where(diagonal, col_recv[turn, 0][None], 0.0), axis=2, keepdims=True)
        east = jnp.sum(jnp.where(diagonal, col_recv[turn, 1][None], 0.0), axis=2, keepdims=True)
        return top, bottom, west, east

    def along(packed, top, bottom, at):
        above = jnp.sum(jnp.where(head, top[:, at : at + 1], 0.0), axis=0, keepdims=True)
        below = jnp.sum(jnp.where(tail, bottom[:, at : at + 1], 0.0), axis=0, keepdims=True)
        up, down = pltpu.roll(packed, 1, 0), pltpu.roll(packed, 7, 0)
        up = jnp.where(row8 == 0, jnp.where(inner == 0, above, pltpu.roll(up, 1, 1)), up)
        down = jnp.where(row8 == 7, jnp.where(inner == per - 1, below, pltpu.roll(down, width - 1, 1)), down)
        return up + down

    def ends(packed):
        return jnp.concatenate(
            [
                jnp.sum(jnp.where(head, packed[0:1], 0.0), axis=1, keepdims=True),
                jnp.sum(jnp.where(tail, packed[7:8], 0.0), axis=1, keepdims=True),
            ],
            axis=0,
        )

    def around(field, l, edges):
        top, bottom, west, east = edges
        x = field[l]
        w = jnp.broadcast_to(west[per * l : per * (l + 1)], (per, 8, width)).reshape(rows, width)
        e = jnp.broadcast_to(east[per * l : per * (l + 1)], (per, 8, width)).reshape(rows, width)
        return (
            jnp.where(lane2 == 0, w, pltpu.roll(x, 1, 1)),
            jnp.where(lane2 == width - 1, e, pltpu.roll(x, width - 1, 1)),
            jnp.where(row2 == 0, top[l : l + 1], pltpu.roll(x, 1, 0)),
            jnp.where(row2 == rows - 1, bottom[l : l + 1], pltpu.roll(x, rows - 1, 0)),
        )

    copies = post(0, border(tracer, 0), column(tracer, 0), column(tracer, width - 1))
    for load in loads[2:]:
        load.wait()
    for l in range(lev):
        inverse = 1.0 / (1.0 + 4.0 * kappa[l])
        scaled[l] = inverse
        coupling[l] = kappa[l] * inverse
    last = lat == bands - 1
    base = pl.multiple_of(jnp.where(last, rows - pole, 0), 8)
    before = jnp.where(last, rows - pole - 1, 0)
    after = jnp.where(last, rows - 1, pole)
    offset = jnp.where(last, (rows - pole) // 8, 0)
    shape = (pole // 8, 8, width)
    lane_p = lax.broadcasted_iota(jnp.int32, (pole, width), 1)
    row_p = lax.broadcasted_iota(jnp.int32, (pole, width), 0)
    for copy in copies:
        copy.wait_recv()
    top, bottom = outer(0)

    def spoke(packed, l):
        mine = lax.broadcasted_iota(jnp.int32, shape, 0) + (per * l + offset) == lax.broadcasted_iota(
            jnp.int32, shape, 2
        )
        value = jnp.sum(jnp.where(mine, packed[None], 0.0), axis=2, keepdims=True)
        return jnp.broadcast_to(value, shape).reshape(pole, width)

    for l in range(lev):
        x = tracer[l, pl.ds(base, pole), :]
        w = jnp.where(lane_p == 0, spoke(col_recv[0, 0], l), pltpu.roll(x, 1, 1))
        e = jnp.where(lane_p == width - 1, spoke(col_recv[0, 1], l), pltpu.roll(x, width - 1, 1))
        above = jnp.where(last, tracer[l, pl.ds(before, 1), :], top[l : l + 1])
        below = jnp.where(last, bottom[l : l + 1], tracer[l, pl.ds(after, 1), :])
        u = jnp.where(row_p == 0, above, pltpu.roll(x, 1, 0))
        d = jnp.where(row_p == pole - 1, below, pltpu.roll(x, pole - 1, 0))
        stage[l] = x - COURANT * 0.5 * (
            wind_east[l, pl.ds(base, pole), :] * (e - w) + wind_north[l, pl.ds(base, pole), :] * (d - u)
        )
    order_out = sorted(range(1, sectors), key=lambda t: abs(t - half))
    rows_out = []
    for t in order_out:
        device = sector(t)
        span = pl.ds(pl.multiple_of(lax.rem(device, slices) * share, 8), share)
        copy = pltpu.make_async_remote_copy(
            src_ref=stage.at[lax.div(device, slices), span, :], dst_ref=spread.at[lon],
            send_sem=a_ss.at[t], recv_sem=a_rs.at[t],
            device_id=(lat, device), device_id_type=pl.DeviceIdType.MESH,
        )
        copy.start()
        rows_out.append(copy)
    sent.extend(rows_out)
    spread[lon] = stage[lax.div(lon, slices), pl.ds(pl.multiple_of(lax.rem(lon, slices) * share, 8), share), :]

    edges = sides(0, top, bottom)
    for l in range(lev):
        w, e, u, d = around(tracer, l, edges)
        filtered[l] = tracer[l] - COURANT * 0.5 * (wind_east[l] * (e - w) + wind_north[l] * (d - u))
    fixed = [(border(a, 0), column(a, 0), column(a, width - 1)) for a in (scaled, coupling)]

    first = jnp.where(lat == bands - 1, pole, 0) + lax.rem(lon, slices) * share
    spot = lax.broadcasted_iota(jnp.int32, (share, 2 * pole), 0) + first
    limit = jnp.sum(
        jnp.where(
            lax.broadcasted_iota(jnp.int32, (share, 2 * pole), 1) == spot,
            cutoff[...].astype(jnp.float32), 0.0,
        ),
        axis=1, keepdims=True,
    )
    kept = 2 * KMAX // sectors
    slot = lax.broadcasted_iota(jnp.int32, (share, 2 * kept), 1)
    wave = sectors * (jnp.where(slot < kept, slot, slot - kept) - kept // 2)
    for copy in rows_out:
        copy.wait_recv()

    def circle(d, k):
        angle = 2.0 * math.pi * ((d * k) % sectors) / sectors
        return math.cos(angle), math.sin(angle)

    even = [spread[0]] + [spread[d] + spread[sectors - d] for d in range(1, half)] + [spread[half]]
    odd = [None] + [spread[d] - spread[sectors - d] for d in range(1, half)]
    blocks = []
    for k in range(half + 1):
        c, s = tw_cos[k : k + 1, :], tw_sin[k : k + 1, :]
        re = weighted([(circle(d, k)[0], even[d]) for d in range(half + 1)])
        im = weighted([(-circle(d, k)[1], odd[d]) for d in range(1, half)])
        if im is None:
            blocks.append(jnp.concatenate([re * c, -(re * s)], axis=1))
        else:
            blocks.append(jnp.concatenate([re * c + im * s, im * c - re * s], axis=1))
    spectrum = jnp.dot(
        jnp.concatenate(blocks, axis=0), fwd[...], precision=HIGHEST, preferred_element_type=jnp.float32
    )
    keep = jnp.concatenate(
        [jnp.where(jnp.abs(wave + k).astype(jnp.float32) <= limit, 1.0, 0.0) for k in range(half + 1)], axis=0
    )
    back = jnp.dot(
        jnp.where(keep > 0.0, spectrum, 0.0), inv[...], precision=HIGHEST, preferred_element_type=jnp.float32
    )
    real, imag = [], []
    for k in range(half + 1):
        c, s = tw_cos[k : k + 1, :], tw_sin[k : k + 1, :]
        zr = back[k * share : (k + 1) * share, :width]
        zi = back[k * share : (k + 1) * share, width:]
        twice = 1.0 if k in (0, half) else 2.0
        real.append((zr * c - zi * s) * twice)
        imag.append((zr * s + zi * c) * twice)
    for d in range(half + 1):
        p = weighted([(circle(d, k)[0], real[k]) for k in range(half + 1)])
        q = weighted([(circle(d, k)[1], imag[k]) for k in range(1, half)])
        if q is None:
            send_b[d] = p
        else:
            send_b[d] = p - q
            send_b[sectors - d] = p + q

    copies = []
    for t in order_out:
        copy = pltpu.make_async_remote_copy(
            src_ref=send_b.at[sector(t)], dst_ref=recv_b.at[lon],
            send_sem=b_ss.at[t], recv_sem=b_rs.at[t],
            device_id=(lat, sector(t)), device_id_type=pl.DeviceIdType.MESH,
        )
        copy.start()
        copies.append(copy)
    sent.extend(copies)
    recv_b[lon] = send_b[lon]
    plain = border(filtered, 0), column(filtered, 0), column(filtered, width - 1)
    polar = (lat == 0) | last
    for copy in copies:
        copy.wait_recv()

    cells = recv_b[...].reshape(lev * pole // 8, 8, width)
    order = lax.broadcasted_iota(jnp.int32, cells.shape, 0)
    order = lax.div(order, pole // 8) * per + offset + lax.rem(order, pole // 8)
    mine = order == lax.broadcasted_iota(jnp.int32, cells.shape, 2)
    step = lax.rem(lane8, per) - offset
    fresh = (step >= 0) & (step < pole // 8) & polar

    def renewed(old, at):
        return jnp.where(fresh, jnp.sum(jnp.where(mine, cells[:, :, at : at + 1], 0.0), axis=0), old)

    rim = jnp.concatenate(
        [recv_b[l * slices, 0:1, :] for l in range(lev)]
        + [recv_b[l * slices + slices - 1, share - 1 : share, :] for l in range(lev)],
        axis=0,
    )
    edge = jnp.where(((row8 < lev) & (lat == 0)) | ((row8 >= lev) & last), rim, plain[0])
    first_column, last_column = renewed(plain[1], 0), renewed(plain[2], width - 1)
    copies = post(1, edge, first_column, last_column)
    fixed[0] = tuple(a * b for a, b in zip(fixed[0], (edge, first_column, last_column)))

    def restore(start):
        for l in range(lev):
            for q in range(slices):
                filtered[l, start + q * share : start + (q + 1) * share, :] = recv_b[l * slices + q]

    @pl.when(lat == 0)
    def _():
        restore(0)

    @pl.when(lat == bands - 1)
    def _():
        restore(rows - pole)

    for l in range(lev):
        scaled[l] = filtered[l] * scaled[l]
    chain = [filtered, ping, pong, ping, balanced]
    for sweep in range(SWEEPS):
        turn, source, target = 1 + sweep, chain[sweep], chain[sweep + 1]
        if sweep < SWEEPS - 1:
            second, second_first, second_last = border(source, 1), column(source, 1), column(source, width - 2)
        for copy in copies:
            copy.wait_recv()
        top, bottom = outer(turn)
        if sweep < SWEEPS - 1:
            west, east = col_recv[turn, 0], col_recv[turn, 1]
            around_edge = (
                jnp.where(lane8 == 0, ends(west), pltpu.roll(edge, 1, 1))
                + jnp.where(lane8 == width - 1, ends(east), pltpu.roll(edge, width - 1, 1))
                + jnp.concatenate([top, bottom], axis=0)
                + second
            )
            around_first = west + second_first + along(first_column, top, bottom, 0)
            around_last = east + second_last + along(last_column, top, bottom, width - 1)
            edge, first_column, last_column = [
                a + b * c for a, b, c in zip(*fixed, (around_edge, around_first, around_last))
            ]
            copies = post(turn + 1, edge, first_column, last_column)
        edges = sides(turn, top, bottom)
        for l in range(lev):
            w, e, u, d = around(source, l, edges)
            target[l] = scaled[l] + coupling[l] * (w + e + u + d)
    for copy in sent:
        copy.wait_send()


def solution(mesh):
    sectors, bands = mesh.shape["lon"], mesh.shape["lat"]

    def per_device(tracer, wind_east, wind_north, kappa, cutoff, partner):
        lev, rows, width = tracer.shape
        share = lev * (cutoff.shape[0] // 2) // sectors
        turns = SWEEPS + 1
        block = pltpu.VMEM((lev, rows, width), jnp.float32)
        vmem = pl.BlockSpec(memory_space=pltpu.VMEM)
        small = (cutoff.reshape(1, -1), partner.reshape(sectors, width), *tables(sectors, width))
        return pl.pallas_call(
            functools.partial(kernel, sectors, bands),
            out_shape=[jax.ShapeDtypeStruct(tracer.shape, jnp.float32)] * 2,
            in_specs=[pl.BlockSpec(memory_space=pltpu.HBM)] * 10,
            out_specs=[vmem] * 2,
            scratch_shapes=[
                block, block, block, block,
                *[pltpu.VMEM(a.shape, a.dtype) for a in small],
                pltpu.SemaphoreType.DMA((10,)),
                pltpu.VMEM((turns, 2, 8, width), jnp.float32),
                pltpu.VMEM((turns, 2, 8, width), jnp.float32),
                pltpu.VMEM((turns, 2 * lev, width), jnp.float32),
                pltpu.VMEM((turns, 4, 2 * lev, width), jnp.float32),
                pltpu.VMEM((lev, cutoff.shape[0] // 2, width), jnp.float32),
                pltpu.VMEM((sectors, share, width), jnp.float32),
                pltpu.VMEM((sectors, share, width), jnp.float32),
                pltpu.VMEM((sectors, share, width), jnp.float32),
                block, block, block, block,
                pltpu.SemaphoreType.DMA((turns, 6)),
                pltpu.SemaphoreType.DMA((turns, 6)),
                pltpu.SemaphoreType.DMA((sectors,)),
                pltpu.SemaphoreType.DMA((sectors,)),
                pltpu.SemaphoreType.DMA((sectors,)),
                pltpu.SemaphoreType.DMA((sectors,)),
            ],
            compiler_params=pltpu.CompilerParams(
                collective_id=0, has_side_effects=True, vmem_limit_bytes=32 * 1024 * 1024
            ),
        )(
            *[pltpu.with_memory_space_constraint(jnp.asarray(a), pltpu.HBM) for a in (tracer, wind_east, wind_north, kappa, *small)]
        )

    spec = P(None, "lat", "lon")
    return jax.shard_map(
        per_device, mesh=mesh, in_specs=(spec, spec, spec, spec, P(), P()), out_specs=(spec, spec),
        check_vma=False,
    )
```

```python
import functools
import math

import jax
import jax.numpy as jnp
import numpy as np
from jax import lax
from jax.experimental import pallas as pl
from jax.experimental.pallas import tpu as pltpu
from jax.sharding import PartitionSpec as P

KMAX = 512
SWEEPS = 4
COURANT = 0.4
HIGHEST = lax.Precision.HIGHEST


def tables(sectors, width):
    total = sectors * width
    half = sectors // 2
    m = np.arange(width)
    theta = 2.0 * np.pi * (np.outer(np.arange(half + 1), m) % total) / total
    kept = 2 * KMAX // sectors
    k2 = np.arange(kept) - kept // 2
    phase = 2.0 * np.pi * (np.outer(m, k2) % width) / width
    c, s = np.cos(phase), np.sin(phase)
    forward = np.block([[c, -s], [s, c]])
    inverse = np.block([[c.T, s.T], [-s.T, c.T]]) / total
    return [a.astype(np.float32) for a in (np.cos(theta), np.sin(theta), forward, inverse)]


def weighted(terms):
    total = None
    for factor, value in terms:
        if abs(factor) < 1e-12:
            continue
        part = value if abs(factor - 1.0) < 1e-12 else value * np.float32(factor)
        total = part if total is None else total + part
    return total


def kernel(
    sectors, bands,
    tracer_h, wind_east_h, wind_north_h, kappa_h, cutoff_h, partner_h, tw_cos_h, tw_sin_h, fwd_h, inv_h,
    filtered, balanced,
    tracer, wind_east, wind_north, kappa, cutoff, partner, tw_cos, tw_sin, fwd, inv, load_s,
    col_send, col_recv, edge_send, edge_recv, stage, spread, send_b, recv_b, coupling, scaled, ping, pong,
    halo_ss, halo_rs, a_ss, a_rs, b_ss, b_rs,
):
    lev, rows, width = tracer.shape
    pole = cutoff.shape[1] // 2
    share = lev * pole // sectors
    slices = sectors // lev
    half = sectors // 2
    groups = lev * rows // 8
    per = rows // 8
    lat = lax.axis_index("lat")
    lon = lax.axis_index("lon")

    def sector(offset):
        return lax.rem(lon + (offset % sectors), sectors)

    def band(offset):
        return lax.rem(lat + (offset % bands), bands)

    held = (tracer_h, partner_h, wind_east_h, wind_north_h, kappa_h, cutoff_h, tw_cos_h, tw_sin_h, fwd_h, inv_h)
    near = (tracer, partner, wind_east, wind_north, kappa, cutoff, tw_cos, tw_sin, fwd, inv)
    loads = [pltpu.make_async_copy(h, v, load_s.at[i]) for i, (h, v) in enumerate(zip(held, near))]
    for load in loads:
        load.start()

    barrier = pltpu.get_barrier_semaphore()
    for t in range(1, sectors):
        pl.semaphore_signal(barrier, inc=1, device_id=(lat, sector(t)), device_id_type=pl.DeviceIdType.MESH)
    beside = (1,) if bands == 2 else (1, -1)
    for t in beside:
        pl.semaphore_signal(barrier, inc=1, device_id=(band(t), lon), device_id_type=pl.DeviceIdType.MESH)
    pl.semaphore_wait(barrier, sectors - 1 + len(beside))

    loads[0].wait()
    loads[1].wait()
    lane2 = lax.broadcasted_iota(jnp.int32, (rows, width), 1)
    row2 = lax.broadcasted_iota(jnp.int32, (rows, width), 0)
    diagonal = lax.broadcasted_iota(jnp.int32, (groups, 8, width), 0) == lax.broadcasted_iota(
        jnp.int32, (groups, 8, width), 2
    )
    reach = partner[pl.ds(lon, 1), :] - sector(half) * width
    reach = jnp.where(reach < 0, reach + sectors * width, reach)
    pick = jnp.where(
        lax.broadcasted_iota(jnp.int32, (2 * width, width), 0) == reach, 1.0, 0.0
    ).astype(jnp.bfloat16)
    lane8 = lax.broadcasted_iota(jnp.int32, (8, width), 1)
    row8 = lax.broadcasted_iota(jnp.int32, (8, width), 0)
    inner = lax.rem(lane8, per)
    level_of = lax.broadcasted_iota(jnp.int32, (lev, width), 0) * per
    place = lax.broadcasted_iota(jnp.int32, (lev, width), 1)
    head, tail = place == level_of, place == level_of + per - 1

    sent = []

    def column(field, at):
        whole = field[...].reshape(groups, 8, width)
        return jnp.sum(jnp.where(diagonal, whole[:, :, at : at + 1], 0.0), axis=0)

    def border(field, depth):
        return jnp.concatenate(
            [field[l, depth : depth + 1, :] for l in range(lev)]
            + [field[l, rows - 1 - depth : rows - depth, :] for l in range(lev)],
            axis=0,
        )

    def post(turn, edge, first_column, last_column):
        edge_send[turn] = edge
        col_send[turn, 0] = last_column
        col_send[turn, 1] = first_column
        plan = [
            (edge_send.at[turn], edge_recv.at[turn, 0], (lat, sector(-half))),
            (edge_send.at[turn], edge_recv.at[turn, 1], (lat, sector(-half - 1))),
            (edge_send.at[turn], edge_recv.at[turn, 2], (band(1), lon)),
            (col_send.at[turn, 0], col_recv.at[turn, 0], (lat, sector(1))),
            (col_send.at[turn, 1], col_recv.at[turn, 1], (lat, sector(-1))),
        ]
        if bands != 2:
            plan.append((edge_send.at[turn], edge_recv.at[turn, 3], (band(-1), lon)))
        copies = []
        for i, (src, dst, device) in enumerate(plan):
            copy = pltpu.make_async_remote_copy(
                src_ref=src, dst_ref=dst, send_sem=halo_ss.at[turn, i], recv_sem=halo_rs.at[turn, i],
                device_id=device, device_id_type=pl.DeviceIdType.MESH,
            )
            copy.start()
            copies.append(copy)
        sent.extend(copies)
        return copies

    def outer(turn):
        x = jnp.concatenate([edge_recv[turn, 0], edge_recv[turn, 1]], axis=1)
        high = x.astype(jnp.bfloat16).astype(jnp.float32)
        rest = x - high
        middle = rest.astype(jnp.bfloat16).astype(jnp.float32)
        parts = jnp.concatenate([high, middle, rest - middle], axis=0).astype(jnp.bfloat16)
        found = jnp.dot(parts, pick, preferred_element_type=jnp.float32)
        n = 2 * lev
        across = found[:n] + found[n : 2 * n] + found[2 * n :]
        top = jnp.where(lat == 0, across[:lev], edge_recv[turn, 2, lev:])
        bottom = jnp.where(lat == bands - 1, across[lev:], edge_recv[turn, 2 if bands == 2 else 3, :lev])
        return top, bottom

    def sides(turn, top, bottom):
        west = jnp.sum(jnp.where(diagonal, col_recv[turn, 0][None], 0.0), axis=2, keepdims=True)
        east = jnp.sum(jnp.where(diagonal, col_recv[turn, 1][None], 0.0), axis=2, keepdims=True)
        return top, bottom, west, east

    def along(packed, top, bottom, at):
        above = jnp.sum(jnp.where(head, top[:, at : at + 1], 0.0), axis=0, keepdims=True)
        below = jnp.sum(jnp.where(tail, bottom[:, at : at + 1], 0.0), axis=0, keepdims=True)
        up, down = pltpu.roll(packed, 1, 0), pltpu.roll(packed, 7, 0)
        up = jnp.where(row8 == 0, jnp.where(inner == 0, above, pltpu.roll(up, 1, 1)), up)
        down = jnp.where(row8 == 7, jnp.where(inner == per - 1, below, pltpu.roll(down, width - 1, 1)), down)
        return up + down

    def ends(packed):
        return jnp.concatenate(
            [
                jnp.sum(jnp.where(head, packed[0:1], 0.0), axis=1, keepdims=True),
                jnp.sum(jnp.where(tail, packed[7:8], 0.0), axis=1, keepdims=True),
            ],
            axis=0,
        )

    def around(field, l, edges):
        top, bottom, west, east = edges
        x = field[l]
        w = jnp.broadcast_to(west[per * l : per * (l + 1)], (per, 8, width)).reshape(rows, width)
        e = jnp.broadcast_to(east[per * l : per * (l + 1)], (per, 8, width)).reshape(rows, width)
        return (
            jnp.where(lane2 == 0, w, pltpu.roll(x, 1, 1)),
            jnp.where(lane2 == width - 1, e, pltpu.roll(x, width - 1, 1)),
            jnp.where(row2 == 0, top[l : l + 1], pltpu.roll(x, 1, 0)),
            jnp.where(row2 == rows - 1, bottom[l : l + 1], pltpu.roll(x, rows - 1, 0)),
        )

    copies = post(0, border(tracer, 0), column(tracer, 0), column(tracer, width - 1))
    for load in loads[2:]:
        load.wait()
    for l in range(lev):
        inverse = 1.0 / (1.0 + 4.0 * kappa[l])
        scaled[l] = inverse
        coupling[l] = kappa[l] * inverse
    last = lat == bands - 1
    base = pl.multiple_of(jnp.where(last, rows - pole, 0), 8)
    before = jnp.where(last, rows - pole - 1, 0)
    after = jnp.where(last, rows - 1, pole)
    offset = jnp.where(last, (rows - pole) // 8, 0)
    shape = (pole // 8, 8, width)
    lane_p = lax.broadcasted_iota(jnp.int32, (pole, width), 1)
    row_p = lax.broadcasted_iota(jnp.int32, (pole, width), 0)
    for copy in copies:
        copy.wait_recv()
    top, bottom = outer(0)

    def spoke(packed, l):
        mine = lax.broadcasted_iota(jnp.int32, shape, 0) + (per * l + offset) == lax.broadcasted_iota(
            jnp.int32, shape, 2
        )
        value = jnp.sum(jnp.where(mine, packed[None], 0.0), axis=2, keepdims=True)
        return jnp.broadcast_to(value, shape).reshape(pole, width)

    def to_share(l, q):
        device = l * slices + q
        return pltpu.make_async_remote_copy(
            src_ref=stage.at[l, pl.ds(q * share, share), :], dst_ref=spread.at[lon],
            send_sem=a_ss.at[device], recv_sem=a_rs.at[lon],
            device_id=(lat, device), device_id_type=pl.DeviceIdType.MESH,
        )

    for l in range(lev):
        x = tracer[l, pl.ds(base, pole), :]
        w = jnp.where(lane_p == 0, spoke(col_recv[0, 0], l), pltpu.roll(x, 1, 1))
        e = jnp.where(lane_p == width - 1, spoke(col_recv[0, 1], l), pltpu.roll(x, width - 1, 1))
        above = jnp.where(last, tracer[l, pl.ds(before, 1), :], top[l : l + 1])
        below = jnp.where(last, bottom[l : l + 1], tracer[l, pl.ds(after, 1), :])
        u = jnp.where(row_p == 0, above, pltpu.roll(x, 1, 0))
        d = jnp.where(row_p == pole - 1, below, pltpu.roll(x, pole - 1, 0))
        stage[l] = x - COURANT * 0.5 * (
            wind_east[l, pl.ds(base, pole), :] * (e - w) + wind_north[l, pl.ds(base, pole), :] * (d - u)
        )
        for q in range(slices):
            @pl.when(lon != l * slices + q)
            def _(l=l, q=q):
                to_share(l, q).start()

            @pl.when(lon == l * slices + q)
            def _(l=l, q=q):
                spread[l * slices + q] = stage[l, q * share : (q + 1) * share, :]

    edges = sides(0, top, bottom)
    for l in range(lev):
        w, e, u, d = around(tracer, l, edges)
        filtered[l] = tracer[l] - COURANT * 0.5 * (wind_east[l] * (e - w) + wind_north[l] * (d - u))
    fixed = [(border(a, 0), column(a, 0), column(a, width - 1)) for a in (scaled, coupling)]

    first = jnp.where(lat == bands - 1, pole, 0) + lax.rem(lon, slices) * share
    spot = lax.broadcasted_iota(jnp.int32, (share, 2 * pole), 0) + first
    limit = jnp.sum(
        jnp.where(
            lax.broadcasted_iota(jnp.int32, (share, 2 * pole), 1) == spot,
            cutoff[...].astype(jnp.float32), 0.0,
        ),
        axis=1, keepdims=True,
    )
    kept = 2 * KMAX // sectors
    slot = lax.broadcasted_iota(jnp.int32, (share, 2 * kept), 1)
    wave = sectors * (jnp.where(slot < kept, slot, slot - kept) - kept // 2)
    for device in range(sectors):
        @pl.when(lon != device)
        def _(device=device):
            pltpu.make_async_remote_copy(
                src_ref=stage.at[device // slices, pl.ds(device % slices * share, share), :],
                dst_ref=spread.at[device], send_sem=a_ss.at[device], recv_sem=a_rs.at[device],
                device_id=(lat, device), device_id_type=pl.DeviceIdType.MESH,
            ).wait()

    def circle(d, k):
        angle = 2.0 * math.pi * ((d * k) % sectors) / sectors
        return math.cos(angle), math.sin(angle)

    even = [spread[0]] + [spread[d] + spread[sectors - d] for d in range(1, half)] + [spread[half]]
    odd = [None] + [spread[d] - spread[sectors - d] for d in range(1, half)]
    blocks = []
    for k in range(half + 1):
        c, s = tw_cos[k : k + 1, :], tw_sin[k : k + 1, :]
        re = weighted([(circle(d, k)[0], even[d]) for d in range(half + 1)])
        im = weighted([(-circle(d, k)[1], odd[d]) for d in range(1, half)])
        if im is None:
            blocks.append(jnp.concatenate([re * c, -(re * s)], axis=1))
        else:
            blocks.append(jnp.concatenate([re * c + im * s, im * c - re * s], axis=1))
    spectrum = jnp.dot(
        jnp.concatenate(blocks, axis=0), fwd[...], precision=HIGHEST, preferred_element_type=jnp.float32
    )
    keep = jnp.concatenate(
        [jnp.where(jnp.abs(wave + k).astype(jnp.float32) <= limit, 1.0, 0.0) for k in range(half + 1)], axis=0
    )
    back = jnp.dot(
        jnp.where(keep > 0.0, spectrum, 0.0), inv[...], precision=HIGHEST, preferred_element_type=jnp.float32
    )
    real, imag = [], []
    for k in range(half + 1):
        c, s = tw_cos[k : k + 1, :], tw_sin[k : k + 1, :]
        zr = back[k * share : (k + 1) * share, :width]
        zi = back[k * share : (k + 1) * share, width:]
        twice = 1.0 if k in (0, half) else 2.0
        real.append((zr * c - zi * s) * twice)
        imag.append((zr * s + zi * c) * twice)
    for d in range(half + 1):
        p = weighted([(circle(d, k)[0], real[k]) for k in range(half + 1)])
        q = weighted([(circle(d, k)[1], imag[k]) for k in range(1, half)])
        if q is None:
            send_b[d] = p
        else:
            send_b[d] = p - q
            send_b[sectors - d] = p + q

    copies = []
    for t in range(1, sectors):
        copy = pltpu.make_async_remote_copy(
            src_ref=send_b.at[sector(t)], dst_ref=recv_b.at[lon],
            send_sem=b_ss.at[t], recv_sem=b_rs.at[t],
            device_id=(lat, sector(t)), device_id_type=pl.DeviceIdType.MESH,
        )
        copy.start()
        copies.append(copy)
    sent.extend(copies)
    recv_b[lon] = send_b[lon]
    plain = border(filtered, 0), column(filtered, 0), column(filtered, width - 1)
    polar = (lat == 0) | last
    for copy in copies:
        copy.wait_recv()

    cells = recv_b[...].reshape(lev * pole // 8, 8, width)
    order = lax.broadcasted_iota(jnp.int32, cells.shape, 0)
    order = lax.div(order, pole // 8) * per + offset + lax.rem(order, pole // 8)
    mine = order == lax.broadcasted_iota(jnp.int32, cells.shape, 2)
    step = lax.rem(lane8, per) - offset
    fresh = (step >= 0) & (step < pole // 8) & polar

    def renewed(old, at):
        return jnp.where(fresh, jnp.sum(jnp.where(mine, cells[:, :, at : at + 1], 0.0), axis=0), old)

    rim = jnp.concatenate(
        [recv_b[l * slices, 0:1, :] for l in range(lev)]
        + [recv_b[l * slices + slices - 1, share - 1 : share, :] for l in range(lev)],
        axis=0,
    )
    edge = jnp.where(((row8 < lev) & (lat == 0)) | ((row8 >= lev) & last), rim, plain[0])
    first_column, last_column = renewed(plain[1], 0), renewed(plain[2], width - 1)
    copies = post(1, edge, first_column, last_column)
    fixed[0] = tuple(a * b for a, b in zip(fixed[0], (edge, first_column, last_column)))

    def restore(start):
        for l in range(lev):
            for q in range(slices):
                filtered[l, start + q * share : start + (q + 1) * share, :] = recv_b[l * slices + q]

    @pl.when(lat == 0)
    def _():
        restore(0)

    @pl.when(lat == bands - 1)
    def _():
        restore(rows - pole)

    for l in range(lev):
        scaled[l] = filtered[l] * scaled[l]
    chain = [filtered, ping, pong, ping, balanced]
    for sweep in range(SWEEPS):
        turn, source, target = 1 + sweep, chain[sweep], chain[sweep + 1]
        if sweep < SWEEPS - 1:
            second, second_first, second_last = border(source, 1), column(source, 1), column(source, width - 2)
        for copy in copies:
            copy.wait_recv()
        top, bottom = outer(turn)
        if sweep < SWEEPS - 1:
            west, east = col_recv[turn, 0], col_recv[turn, 1]
            around_edge = (
                jnp.where(lane8 == 0, ends(west), pltpu.roll(edge, 1, 1))
                + jnp.where(lane8 == width - 1, ends(east), pltpu.roll(edge, width - 1, 1))
                + jnp.concatenate([top, bottom], axis=0)
                + second
            )
            around_first = west + second_first + along(first_column, top, bottom, 0)
            around_last = east + second_last + along(last_column, top, bottom, width - 1)
            edge, first_column, last_column = [
                a + b * c for a, b, c in zip(*fixed, (around_edge, around_first, around_last))
            ]
            copies = post(turn + 1, edge, first_column, last_column)
        edges = sides(turn, top, bottom)
        for l in range(lev):
            w, e, u, d = around(source, l, edges)
            target[l] = scaled[l] + coupling[l] * (w + e + u + d)
    for copy in sent:
        copy.wait_send()


def solution(mesh):
    sectors, bands = mesh.shape["lon"], mesh.shape["lat"]

    def per_device(tracer, wind_east, wind_north, kappa, cutoff, partner):
        lev, rows, width = tracer.shape
        share = lev * (cutoff.shape[0] // 2) // sectors
        turns = SWEEPS + 1
        block = pltpu.VMEM((lev, rows, width), jnp.float32)
        vmem = pl.BlockSpec(memory_space=pltpu.VMEM)
        small = (cutoff.reshape(1, -1), partner.reshape(sectors, width), *tables(sectors, width))
        return pl.pallas_call(
            functools.partial(kernel, sectors, bands),
            out_shape=[jax.ShapeDtypeStruct(tracer.shape, jnp.float32)] * 2,
            in_specs=[pl.BlockSpec(memory_space=pltpu.HBM)] * 10,
            out_specs=[vmem] * 2,
            scratch_shapes=[
                block, block, block, block,
                *[pltpu.VMEM(a.shape, a.dtype) for a in small],
                pltpu.SemaphoreType.DMA((10,)),
                pltpu.VMEM((turns, 2, 8, width), jnp.float32),
                pltpu.VMEM((turns, 2, 8, width), jnp.float32),
                pltpu.VMEM((turns, 2 * lev, width), jnp.float32),
                pltpu.VMEM((turns, 4, 2 * lev, width), jnp.float32),
                pltpu.VMEM((lev, cutoff.shape[0] // 2, width), jnp.float32),
                pltpu.VMEM((sectors, share, width), jnp.float32),
                pltpu.VMEM((sectors, share, width), jnp.float32),
                pltpu.VMEM((sectors, share, width), jnp.float32),
                block, block, block, block,
                pltpu.SemaphoreType.DMA((turns, 6)),
                pltpu.SemaphoreType.DMA((turns, 6)),
                pltpu.SemaphoreType.DMA((sectors,)),
                pltpu.SemaphoreType.DMA((sectors,)),
                pltpu.SemaphoreType.DMA((sectors,)),
                pltpu.SemaphoreType.DMA((sectors,)),
            ],
            compiler_params=pltpu.CompilerParams(
                collective_id=0, has_side_effects=True, vmem_limit_bytes=32 * 1024 * 1024
            ),
        )(
            *[pltpu.with_memory_space_constraint(jnp.asarray(a), pltpu.HBM) for a in (tracer, wind_east, wind_north, kappa, *small)]
        )

    spec = P(None, "lat", "lon")
    return jax.shard_map(
        per_device, mesh=mesh, in_specs=(spec, spec, spec, spec, P(), P()), out_specs=(spec, spec),
        check_vma=False,
    )
```
